256 devices in a mesh: rep: 8 (over y_hi, x), ep: 32 (over z, y_lo, core).
Axes of the slice: x: 4, y: 4 (y_hi: 2, y_lo: 2; y = y_hi * 2 + y_lo), z: 8, core: 2. Of those that a mesh axis runs over, the one named last changes fastest.
Arguments:
- tokens: bfloat16 [32768, 1024], P(('rep', 'ep')), may hold values from -6 to 6
- expert_ids: int32 [32768, 4], P(('rep', 'ep')), may hold values from 0 to 31, all different within a row; in each aligned block of 128 rows (0 to 127, 128 to 255, ...) at most 32 rows name the same one
- gate_probs: float32 [32768, 4], P(('rep', 'ep')), may hold values from 0.05 to 1
- out_grad: bfloat16 [32768, 1024], P(('rep', 'ep')), may hold values from -0.75 to 0.75
- w_in: bfloat16 [32, 1024, 1024], P('ep'), may hold values from -0.1875 to 0.1875
- w_out: bfloat16 [32, 1024, 1024], P('ep'), may hold values from -0.1875 to 0.1875
Outputs:
- mixed: bfloat16 [32768, 1024], P(('rep', 'ep'))
- token_grad: bfloat16 [32768, 1024], P(('rep', 'ep'))
- gate_grad: float32 [32768, 4], P(('rep', 'ep'))
- in_weight_grad: float32 [32, 1024, 1024], P('ep', 'rep')
- out_weight_grad: float32 [32, 1024, 1024], P('ep', 'rep')
The draws below stay inside these ranges and needn't reach their ends.
Inputs may be any that keep to these rules, and one draw needn't show every extreme that they name: `expert_ids`: each token names 4 different experts. Within each device's block of 128 tokens no expert is named by more than 32 tokens, and in every draw some expert is named by exactly 32 tokens of some block.
All inputs are finite; a program needn't handle non-finite values.
Results may differ from the reference program's by a relative error of at most 0.014.
Values may be sent and summed in bfloat16 or wider, within the bound.
A program may use at most 64 MiB of HBM per device.

```python
import math
import jax
import jax.numpy as jnp
import numpy as np
from jax import lax

D = 1024
H = 1024
TOPK = 4
TOK_DEV = 128
EXPERTS = 32
CAP = 32
TOKENS = 32768
N_REP = 8
N_EP = 32


def level_of(own_key, shape, split, least, top_value):
    def one(dim, shards_of):
        heights = jax.random.uniform(jax.random.fold_in(jax.random.fold_in(own_key, 6), dim), (shards_of,), jnp.float32, least / len(split), top_value / len(split))
        return jnp.repeat(jnp.exp(heights), shape[dim] // shards_of).reshape((-1,) + (1,) * (len(shape) - dim - 1))

    factor_of = one(*split[0])
    for cut in split[1:]:
        factor_of = factor_of * one(*cut)
    return factor_of


def shared_out(stream_key, own, number, rows, number_of, top, bound, slope):
    order = jax.random.permutation(stream_key, number_of)
    packed, usual = shares(number_of, rows * top, bound, slope, True), shares(number_of, rows * top, bound, slope, False)
    places = jnp.arange(number_of)

    def named(tallies, offset_by):
        used = int((tallies > 0).sum())
        fixed = max(1, used // 4)
        passed = fixed + (places - fixed + offset_by * (used - fixed)) % max(1, number_of - fixed)
        return jnp.zeros((number_of,), jnp.int32).at[order[jnp.where(places < fixed, places, passed)]].set(jnp.asarray(tallies, jnp.int32))

    tallies = jnp.where(number % 4 == 0, named(packed, number // 4), named(usual, number - number // 4 - 1))
    mixed = jax.random.permutation(jax.random.fold_in(own, 3), number_of)
    giver, receiver = mixed[0:number_of // 2 * 2:2], mixed[1:number_of // 2 * 2:2]
    slack = jnp.minimum(tallies[giver] - 1, bound - tallies[receiver]) // 2
    slack = jnp.where((giver == order[0]) | (receiver == order[0]) | (tallies[receiver] == 0), 0, jnp.maximum(slack, 0))
    passed = jax.random.randint(jax.random.fold_in(own, 4), (number_of // 2,), 0, 1 << 20) % (slack + 1)
    tallies = tallies.at[giver].add(-passed).at[receiver].add(passed)
    labels = jnp.searchsorted(jnp.cumsum(tallies), jnp.arange(rows * top), side="right").astype(jnp.int32)
    grid = labels.reshape(top, rows).T
    grid = grid[jax.random.permutation(jax.random.fold_in(own, 1), rows)]
    offset_by = jax.random.randint(jax.random.fold_in(own, 2), (rows, 1), 0, top)
    return jnp.take_along_axis(grid, (jnp.arange(top)[None, :] + offset_by) % top, axis=1)


def shares(number_of, total, reach, lean, full):
    loads = [(1 << 20) // math.isqrt(standing ** lean) + 1 for standing in range(1, number_of + 1)]
    largest = reach if full else min(reach, max(-(-total // number_of), total * loads[0] // sum(loads)))
    least = 1 if total - largest >= number_of - 1 else 0
    counts, surplus = [largest] + [least] * (number_of - 1), total - largest - least * (number_of - 1)
    while surplus > 0:
        candidates = [i for i in range(1, number_of) if counts[i] < largest] or [i for i in range(1, number_of) if counts[i] < reach]
        whole, left = sum([loads[i] for i in candidates]), surplus
        for i in candidates:
            addition = min(reach - counts[i], max(1, left * loads[i] // whole), surplus)
            counts[i] = counts[i] + addition
            surplus = surplus - addition
    return np.array(counts)


def scatter_about(own_key, extent, width, limit, pieces=(), kind=jnp.bfloat16):
    array = jax.random.normal(own_key, extent, jnp.float32) * width
    if len(pieces) > 0:
        array = level_of(own_key, extent, pieces, -0.22, 0.18) * array
    return jnp.clip(array, min=-limit, max=limit).astype(kind)


def setup_inputs(seed: int = 0) -> dict:
    key_list = jax.random.split(jax.random.key(seed), 7)
    tokens = scatter_about(key_list[0], (TOKENS, D), 1.0, 6.0, ((0, 256),))
    expert_ids_keys = jax.random.split(jax.random.fold_in(key_list[1], 1), TOKENS // TOK_DEV)
    expert_ids_turns = jax.random.permutation(jax.random.fold_in(key_list[1], 3), TOKENS // TOK_DEV)
    expert_ids = jax.vmap(lambda own, number: shared_out(jax.random.fold_in(key_list[1], 2), own, number, TOK_DEV, EXPERTS, TOPK, CAP, 2))(expert_ids_keys, expert_ids_turns).reshape((TOKENS, TOPK))
    gate_probs = jnp.clip(jnp.exp(math.log(1.0) - 2.9957323 * jax.random.uniform(key_list[2], (TOKENS, TOPK), jnp.float32) ** level_of(key_list[2], (TOKENS, TOPK), ((0, 256),), -0.2, 0.2)), 0.05, 1.0)
    out_grad = scatter_about(key_list[3], (TOKENS, D), 0.125, 0.75, ((0, 256),))
    w_in = scatter_about(key_list[4], (EXPERTS, D, H), D ** -0.5, 0.1875, ((0, 32),))
    w_out = scatter_about(key_list[5], (EXPERTS, H, D), H ** -0.5, 0.1875, ((0, 32),))
    return dict(tokens=tokens, expert_ids=expert_ids, gate_probs=gate_probs, out_grad=out_grad, w_in=w_in, w_out=w_out)


ROOT_HALF = 0.7071067811865476
INV_ROOT_TAU = 0.3989422804014327


def gelu_value(preact):
    return 0.5 * preact * (1.0 + lax.erf(preact * ROOT_HALF))


def gelu_slope(preact):
    return 0.5 * (1.0 + lax.erf(preact * ROOT_HALF)) + preact * INV_ROOT_TAU * jnp.exp(-0.5 * preact * preact)


def block_targets(block_ids):
    onehot = (block_ids[:, None] == jnp.arange(EXPERTS, dtype=jnp.int32)[None, :]).astype(jnp.int32)
    earlier = jnp.cumsum(onehot, axis=0) - onehot
    return (block_ids * CAP + jnp.sum(earlier * onehot, axis=1)).astype(jnp.int32)


def place_block(rows, target):
    return jnp.zeros((EXPERTS * CAP, rows.shape[1]), rows.dtype).at[target].set(rows)


def pick_rows(table, target):
    return table[target]


def reference(tokens, expert_ids, gate_probs, out_grad, w_in, w_out):
    toks = tokens.reshape(N_REP, N_EP, TOK_DEV, D)
    ids = expert_ids.reshape(N_REP, N_EP, TOK_DEV * TOPK)
    probs = gate_probs.reshape(N_REP, N_EP, TOK_DEV, TOPK)
    grads = out_grad.reshape(N_REP, N_EP, TOK_DEV, D)
    w_in_wide = w_in.astype(jnp.float32)
    w_out_wide = w_out.astype(jnp.float32)

    def one_group(carry, inputs):
        in_sum, out_sum = carry
        toks_group, ids_group, probs_group, grads_group = inputs
        target = jax.vmap(block_targets)(ids_group)
        x_rows = jnp.repeat(toks_group, TOPK, axis=1)
        g_rows = (probs_group.reshape(N_EP, TOK_DEV * TOPK)[:, :, None]
                  * jnp.repeat(grads_group, TOPK, axis=1).astype(jnp.float32)).astype(jnp.bfloat16)
        x_sent = jax.vmap(place_block)(x_rows, target).reshape(N_EP, EXPERTS, CAP, D)
        g_sent = jax.vmap(place_block)(g_rows, target).reshape(N_EP, EXPERTS, CAP, D)
        arrived = jnp.transpose(x_sent, (1, 0, 2, 3)).astype(jnp.float32)
        out_rows = jnp.transpose(g_sent, (1, 0, 2, 3)).astype(jnp.float32)
        preact = jnp.einsum("escd,edh->esch", arrived, w_in_wide)
        activated = gelu_value(preact).astype(jnp.bfloat16).astype(jnp.float32)
        expert_out = jnp.einsum("esch,ehd->escd", activated, w_out_wide).astype(jnp.bfloat16)
        act_grad = jnp.einsum("escd,ehd->esch", out_rows, w_out_wide)
        pre_grad = (act_grad * gelu_slope(preact)).astype(jnp.bfloat16).astype(jnp.float32)
        row_grads = jnp.einsum("esch,edh->escd", pre_grad, w_in_wide).astype(jnp.bfloat16)
        in_part = lax.optimization_barrier(jnp.einsum("escd,esch->edh", arrived, pre_grad).astype(jnp.bfloat16)).astype(jnp.float32)
        out_part = lax.optimization_barrier(jnp.einsum("esch,escd->ehd", activated, out_rows).astype(jnp.bfloat16)).astype(jnp.float32)
        back_out = jnp.transpose(expert_out, (1, 0, 2, 3)).reshape(N_EP, EXPERTS * CAP, D)
        back_grad = jnp.transpose(row_grads, (1, 0, 2, 3)).reshape(N_EP, EXPERTS * CAP, D)
        picked = jax.vmap(pick_rows)(back_out, target).reshape(N_EP, TOK_DEV, TOPK, D).astype(jnp.float32)
        picked_grad = jax.vmap(pick_rows)(back_grad, target).reshape(N_EP, TOK_DEV, TOPK, D).astype(jnp.float32)
        mixed = jnp.sum(probs_group[:, :, :, None] * picked, axis=2).astype(jnp.bfloat16)
        gate_grad = jnp.sum(grads_group.astype(jnp.float32)[:, :, None, :] * picked, axis=3)
        token_grad = jnp.sum(picked_grad, axis=2).astype(jnp.bfloat16)
        return (in_sum + in_part, out_sum + out_part), (mixed, token_grad, gate_grad)

    start = (jnp.zeros((EXPERTS, D, H), jnp.float32), jnp.zeros((EXPERTS, H, D), jnp.float32))
    sums, results = lax.scan(one_group, start, (toks, ids, probs, grads))
    mixed, token_grad, gate_grad = results
    return (mixed.reshape(TOKENS, D), token_grad.reshape(TOKENS, D),
            gate_grad.reshape(TOKENS, TOPK), sums[0], sums[1])
```

```python
import jax
import jax.numpy as jnp
from jax import lax
from jax.experimental import pallas as pl
from jax.experimental.pallas import tpu as pltpu
from jax.sharding import PartitionSpec as P

MESH = pl.DeviceIdType.MESH
BF = jnp.bfloat16
F32 = jnp.float32
NZ, NX = 8, 4
T = 128
HALF = 64
CAP = 32
D = 1024
ROOT_HALF = 0.7071067811865476
INV_ROOT_TAU = 0.3989422804014327

ORDER = (0, 7, 1, 6, 2, 5, 3, 4)
POS = {r: p for p, r in enumerate(ORDER)}
RS_UNITS = (
    ((0, 4), (1, 3), (0, 3), (1, 2), (0, 2), (1, 1), (0, 1)),
    ((1, 4), (0, 5), (1, 5), (0, 6), (1, 6), (0, 7), (1, 7)),
)


def dot(a, b, dims=((1,), (0,))):
    return lax.dot_general(a, b, (dims, ((), ())), preferred_element_type=F32)


def kernel(
    tok, grd, meta, win, wout,
    mixed_o, tgrad_o, gg_o, gin_o, gout_o,
    ball, metall, sel, selt, gatet, gslot, wi, wo,
    disp, arr, act, slope, pre, res, ret,
    rs_send, rs_recv, gg_send, gg_recv,
    wx_send, wx_recv, wx_own, wx_chain, wy_send, wy_recv,
    loc_sem, ag_s, ag_r, meta_s, meta_r, disp_s, disp_r, ret_s, ret_r,
    rs_s, rs_r, gg_s, gg_r, wx_s, wx_r, wy_s, wy_r,
):
    rep = lax.axis_index("rep")
    ep = lax.axis_index("ep")
    x, y_hi = lax.rem(rep, 4), lax.div(rep, 4)
    c, y_lo, z = lax.rem(ep, 2), lax.rem(lax.div(ep, 2), 2), lax.div(ep, 4)
    y = y_hi * 2 + y_lo

    def dev(x_, y_, z_, c_):
        return (lax.div(y_, 2) * 4 + x_, (z_ * 2 + lax.rem(y_, 2)) * 2 + c_)

    def along_z(r):
        return dev(x, y, lax.rem(z + r, 8), c)

    y_up, y_dn = lax.rem(y + 1, 4), lax.rem(y + 3, 4)
    y_to = lax.rem(y + 1 + 2 * c, 4)
    y_from_other = lax.rem(y + 1 + 2 * c, 4)
    y_from_same = lax.rem(y + 3 - 2 * c, 4)
    other = 1 - c
    to_plane = (None, dev(x, y, z, other), dev(x, y_to, z, c), dev(x, y_to, z, other))
    from_plane = (
        None, dev(x, y, z, other), dev(x, y_from_same, z, c), dev(x, y_from_other, z, other),
    )
    x_right, x_left = dev(lax.rem(x + 1, 4), y, z, c), dev(lax.rem(x + 3, 4), y, z, c)
    y_far = dev(x, lax.rem(y + 2, 4), z, c)
    partners = [along_z(r) for r in range(1, 8)]
    partners += [to_plane[1], to_plane[2], to_plane[3], from_plane[2]]
    partners += [x_right, x_left, y_far]

    sent = []

    def rcopy(src, dst, ss, rs, device):
        return pltpu.make_async_remote_copy(
            src_ref=src, dst_ref=dst, send_sem=ss, recv_sem=rs, device_id=device, device_id_type=MESH
        )

    def go(copy):
        copy.start()
        sent.append(copy)

    local = {}

    def lcopy(name, src, dst, i):
        local[name] = pltpu.make_async_copy(src, dst, loc_sem.at[i])
        local[name].start()

    lcopy("x", tok, ball.at[0, 0], 0)
    lcopy("m", meta, metall.at[0], 2)
    lcopy("wi", win.at[0], wi, 3)
    lcopy("wo", wout.at[0], wo, 4)
    lcopy("g", grd, ball.at[1, 0], 1)

    barrier = pltpu.get_barrier_semaphore()
    for p in partners:
        pl.semaphore_signal(barrier, inc=1, device_id=p, device_id_type=MESH)
    pl.semaphore_wait(barrier, len(partners))

    own = (tok, grd)

    def ag(a, d, h, half):
        rows = pl.ds(half * HALF, HALF)
        if h == 1:
            src = own[a].at[rows]
        else:
            src = ball.at[a, 8 - (h - 1) if d == 0 else h - 1, rows]
        dst = ball.at[a, 8 - h if d == 0 else h, rows]
        return rcopy(src, dst, ag_s.at[a, d, h - 1, half], ag_r.at[a, d, h - 1, half],
                     along_z(1 if d == 0 else 7))

    def ag_own(a):
        for i in range(2):
            go(ag(a, 0, 1, i))
            go(ag(a, 1, 1, 1 - i))

    def ag_relay(a, h, i):
        for d in range(2):
            half = d if i == 0 else 1 - d
            ag(a, d, h, half).wait_recv()
            if h < (4 if i == 0 else 3):
                go(ag(a, d, h + 1, half))

    def meta_copy(r):
        return rcopy(meta, metall.at[8 - r], meta_s.at[8 - r], meta_r.at[8 - r], along_z(r))

    ag_own(0)
    for r in (1, 7, 2, 6, 3, 5, 4):
        go(meta_copy(r))

    row = lax.broadcasted_iota(jnp.int32, (T, T), 0)
    q = lax.div(row, CAP)
    q_c = lax.rem(c + lax.rem(q, 2), 2)
    q_y = lax.rem(y_lo + lax.div(q, 2), 2)
    row_place = (((z * 2 + q_y) * 2 + q_c) * CAP + lax.rem(row, CAP)).astype(F32)

    def onehots(r):
        m = metall[r]
        return [jnp.where(m[k:k + 1, :] == row_place, 1.0, 0.0) for k in range(4)], m

    def build(r):
        if r == 0:
            local["m"].wait()
        else:
            meta_copy(8 - r).wait_recv()
        hots, m = onehots(r)
        total = hots[0] + hots[1] + hots[2] + hots[3]
        gated = sum(hots[k] * m[4 + k:5 + k, :] for k in range(4))
        sel[r] = total.astype(BF)
        selt[r] = total.T.astype(BF)
        gatet[r] = gated.T.astype(BF)
        gslot[r] = jnp.broadcast_to(jnp.sum(gated, axis=1, keepdims=True), (T, T))

    def disp_copy(a, r, k):
        p = POS[r]
        return rcopy(disp.at[a, p, k - 1], arr.at[a, p, k], disp_s.at[a, p, k], disp_r.at[a, p, k],
                     to_plane[k])

    def dispatch(a, r):
        if r == 0:
            local["x" if a == 0 else "g"].wait()
        rows = dot(sel[r], ball[a, r])
        if a == 1:
            rows = rows * gslot[r][:, 0:1]
        rows = rows.astype(BF)
        p = POS[r]
        for k in (2, 3, 1):
            disp[a, p, k - 1] = rows[k * CAP:(k + 1) * CAP]
            go(disp_copy(a, r, k))
        arr[a, p, 0] = rows[:CAP]

    def ret_copy(a, p, k):
        return rcopy(res.at[a, p, k], ret.at[a, p, k], ret_s.at[a, p, k], ret_r.at[a, p, k],
                     from_plane[k])

    def give_back(a, j):
        for p in (2 * j, 2 * j + 1):
            for k in (2, 3, 1):
                go(ret_copy(a, p, k))
            ret[a, p, 0] = res[a, p, 0]

    def await_rows(a, j):
        for p in (2 * j, 2 * j + 1):
            for k in (1, 2, 3):
                disp_copy(a, ORDER[p], k).wait_recv()

    def forward(j):
        await_rows(0, j)
        rows = arr[0, 2 * j:2 * j + 2].reshape(256, D)

        def tile(n, _):
            cols = pl.ds(pl.multiple_of(n * 256, 256), 256)
            v = dot(rows, wi[:, cols])
            half_one = 0.5 * (1.0 + lax.erf(v * ROOT_HALF))
            act[pl.ds(256 * j, 256), cols] = (v * half_one).astype(BF)
            slope[pl.ds(256 * j, 256), cols] = half_one + v * INV_ROOT_TAU * jnp.exp(-0.5 * v * v)
            return 0

        lax.fori_loop(0, 4, tile, 0)
        hidden = act[pl.ds(256 * j, 256), :]

        def tile_out(n, _):
            cols = pl.ds(pl.multiple_of(n * 256, 256), 256)
            res[0, 2 * j:2 * j + 2, :, :, cols] = (
                dot(hidden, wo[:, cols]).astype(BF).reshape(2, 4, CAP, 256)
            )
            return 0

        lax.fori_loop(0, 4, tile_out, 0)
        give_back(0, j)

    def backward(j):
        rows = arr[1, 2 * j:2 * j + 2].reshape(256, D)

        def tile(n, _):
            cols = pl.ds(pl.multiple_of(n * 256, 256), 256)
            v = dot(rows, wo[cols, :], ((1,), (1,)))
            pre[pl.ds(256 * j, 256), cols] = (v * slope[pl.ds(256 * j, 256), cols]).astype(BF)
            return 0

        lax.fori_loop(0, 4, tile, 0)
        hidden = pre[pl.ds(256 * j, 256), :]

        def tile_out(n, _):
            cols = pl.ds(pl.multiple_of(n * 256, 256), 256)
            res[1, 2 * j:2 * j + 2, :, :, cols] = (
                dot(hidden, wi[cols, :], ((1,), (1,))).astype(BF).reshape(2, 4, CAP, 256)
            )
            return 0

        lax.fori_loop(0, 4, tile_out, 0)
        give_back(1, j)

    returned = set()

    def combine(a, r, half):
        p = POS[r]
        if (a, p) not in returned:
            returned.add((a, p))
            for k in (1, 2, 3):
                ret_copy(a, p, k).wait_recv()
        weights = (gatet if a == 0 else selt)[r, half * HALF:(half + 1) * HALF]
        return dot(weights, ret[a, p].reshape(T, D))

    def rs_copy(a, d, i):
        return rcopy(rs_send.at[a, d, i], rs_recv.at[a, d, i], rs_s.at[a, d, i], rs_r.at[a, d, i],
                     along_z(1 if d == 0 else 7))

    def rs(a, i):
        for d in range(2):
            half, r = RS_UNITS[d][i]
            prior = (half, r + 1 if d == 0 else r - 1)
            total = combine(a, r, half)
            if prior in RS_UNITS[d]:
                n = RS_UNITS[d].index(prior)
                rs_copy(a, d, n).wait_recv()
                total = total + rs_recv[a, d, n].astype(F32)
            rs_send[a, d, i] = total.astype(BF)
            go(rs_copy(a, d, i))

    def rs_end(a, out):
        for half in range(2):
            total = combine(a, 0, half)
            for d in range(2):
                n = RS_UNITS[d].index((half, 1 if d == 0 else 7))
                rs_copy(a, d, n).wait_recv()
                total = total + rs_recv[a, d, n].astype(F32)
            out[half * HALF:(half + 1) * HALF, :] = total.astype(BF)

    def gg_copy(r):
        return rcopy(gg_send.at[r], gg_recv.at[r], gg_s.at[r], gg_r.at[r], along_z(r))

    def gate_grad(r):
        m = dot(ret[0, POS[r]].reshape(T, D), ball[1, r], ((1,), (1,)))
        hots, _ = onehots(r)
        out = gg_send if r else gg_recv
        for k in range(4):
            out[r, k:k + 1, :] = jnp.sum(m * hots[k], axis=0, keepdims=True)
        if r:
            out[r, 4:8, :] = jnp.zeros((4, T), F32)
            go(gg_copy(r))

    def wx_copy(w, i):
        return rcopy(wx_send.at[w, i], wx_recv.at[w, i], wx_s.at[w, i], wx_r.at[w, i],
                     x_right if i < 3 else x_left)

    def wgrad(w, dx):
        lhs_ref, rhs = (act, arr.at[1]) if w == 1 else (arr.at[0], pre)
        dest = lax.rem(x + dx, 4)
        parts = []
        for yh in range(2):
            cols = pl.ds(pl.multiple_of((yh * 4 + dest) * 128, 128), 128)
            if w == 1:
                parts.append(act[:, cols])
            else:
                parts.append(arr[0, :, :, :, cols].reshape(1024, 128))
        lhs = jnp.concatenate(parts, axis=1)

        def tile(n, _):
            cols = pl.ds(pl.multiple_of(n * 256, 256), 256)
            if w == 1:
                right = arr[1, :, :, :, cols].reshape(1024, 256)
            else:
                right = pre[:, cols]
            v = dot(lhs, right, ((0,), (0,)))
            a, b = v[:128], v[128:]
            if dx == 2:
                wx_send[w, 3, :, cols] = a.astype(BF)
                wx_send[w, 0, :, cols] = b.astype(BF)
            elif dx == 1:
                wx_send[w, 1, :, cols] = a.astype(BF)
                wx_chain[w, 0, :, cols] = b
            elif dx == 3:
                wx_send[w, 4, :, cols] = b.astype(BF)
                wx_chain[w, 1, :, cols] = a
            else:
                wx_own[w, 0, :, cols] = a
                wx_own[w, 1, :, cols] = b
            return 0

        lax.fori_loop(0, 4, tile, 0)
        for i in {2: (3, 0), 1: (1,), 3: (4,), 0: ()}[dx]:
            go(wx_copy(w, i))

    def wchain(w):
        for i, first, n in ((2, 0, 0), (5, 3, 1)):
            wx_copy(w, first).wait_recv()
            wx_send[w, i] = (wx_chain[w, n] + wx_recv[w, first].astype(F32)).astype(BF)
            go(wx_copy(w, i))

    def wy_copy(w):
        return rcopy(wy_send.at[w], wy_recv.at[w], wy_s.at[w], wy_r.at[w], y_far)

    def wsum(w):
        for i in (1, 2, 4, 5):
            wx_copy(w, i).wait_recv()
        wx_own[w, 0] = wx_own[w, 0] + wx_recv[w, 1].astype(F32) + wx_recv[w, 5].astype(F32)
        wx_own[w, 1] = wx_own[w, 1] + wx_recv[w, 2].astype(F32) + wx_recv[w, 4].astype(F32)
        wy_send[w] = wx_own[w, 1 - y_hi].astype(BF)
        go(wy_copy(w))

    def wend(w, out):
        wy_copy(w).wait_recv()
        out[...] = wx_own[w, y_hi] + wy_recv[w].astype(F32)

    build(0)
    dispatch(0, 0)
    ag_relay(0, 1, 0)
    ag_relay(0, 1, 1)
    build(7)
    build(1)
    dispatch(0, 7)
    dispatch(0, 1)
    ag_relay(0, 2, 0)
    local["wi"].wait()
    local["wo"].wait()
    forward(0)
    ag_relay(0, 2, 1)
    build(6)
    build(2)
    dispatch(0, 6)
    dispatch(0, 2)
    ag_relay(0, 3, 0)
    ag_own(1)
    forward(1)
    ag_relay(0, 3, 1)
    build(5)
    build(3)
    dispatch(0, 5)
    dispatch(0, 3)
    forward(2)
    ag_relay(0, 4, 0)
    build(4)
    dispatch(0, 4)
    dispatch(1, 0)
    ag_relay(1, 1, 0)
    forward(3)
    ag_relay(1, 1, 1)
    dispatch(1, 7)
    dispatch(1, 1)
    ag_relay(1, 2, 0)
    await_rows(1, 0)
    backward(0)
    ag_relay(1, 2, 1)
    dispatch(1, 6)
    dispatch(1, 2)
    ag_relay(1, 3, 0)
    rs(0, 0)
    rs(0, 1)
    await_rows(1, 1)
    backward(1)
    ag_relay(1, 3, 1)
    dispatch(1, 5)
    dispatch(1, 3)
    await_rows(1, 2)
    backward(2)
    ag_relay(1, 4, 0)
    dispatch(1, 4)
    await_rows(1, 3)
    wgrad(1, 2)
    rs(0, 2)
    wgrad(1, 1)
    wgrad(1, 3)
    rs(0, 3)
    backward(3)
    wgrad(1, 0)
    rs(0, 4)
    wgrad(0, 2)
    wchain(1)
    rs(0, 5)
    wgrad(0, 1)
    wgrad(0, 3)
    rs(0, 6)
    rs(1, 0)
    rs(1, 1)
    wgrad(0, 0)
    for r in (4, 3, 5, 2, 6, 1, 7, 0):
        if r == 0:
            combined = [combine(0, 0, 0)]
        gate_grad(r)
    wchain(0)
    rs(1, 2)
    rs_end(0, mixed_o)
    rs(1, 3)
    wsum(1)
    rs(1, 4)
    rs(1, 5)
    wsum(0)
    rs(1, 6)
    for r in range(1, 8):
        gg_copy(r).wait_recv()
    gg = gg_recv[0]
    for r in range(1, 8):
        gg = gg + gg_recv[r]
    gg_o[...] = gg
    wend(1, gout_o)
    rs_end(1, tgrad_o)
    wend(0, gin_o)
    for copy in sent:
        copy.wait_send()


def places(expert_ids):
    experts = jnp.arange(32, dtype=jnp.int32)
    hot = (expert_ids[:, :, None] == experts).astype(jnp.int32)
    named = jnp.sum(hot, axis=1)
    before = jnp.tril(jnp.ones((T, T), F32), -1) @ named.astype(F32)
    slot = jnp.sum(before[:, None, :] * hot.astype(F32), axis=2)
    return expert_ids.astype(F32) * CAP + slot


def body(tokens, expert_ids, gate_probs, out_grad, w_in, w_out):
    meta = jnp.concatenate([places(expert_ids).T, gate_probs.T], axis=0)
    anyspec = pl.BlockSpec(memory_space=pl.ANY)
    vmem = pl.BlockSpec(memory_space=pltpu.VMEM)
    dma = pltpu.SemaphoreType.DMA
    scratch = [
        pltpu.VMEM((2, 8, T, D), BF),
        pltpu.VMEM((8, 8, T), F32),
        pltpu.VMEM((8, T, T), BF),
        pltpu.VMEM((8, T, T), BF),
        pltpu.VMEM((8, T, T), BF),
        pltpu.VMEM((8, T, T), F32),
        pltpu.VMEM((D, D), BF),
        pltpu.VMEM((D, D), BF),
        pltpu.VMEM((2, 8, 3, CAP, D), BF),
        pltpu.VMEM((2, 8, 4, CAP, D), BF),
        pltpu.VMEM((1024, D), BF),
        pltpu.VMEM((1024, D), F32),
        pltpu.VMEM((1024, D), BF),
        pltpu.VMEM((2, 8, 4, CAP, D), BF),
        pltpu.VMEM((2, 8, 4, CAP, D), BF),
        pltpu.VMEM((2, 2, 7, HALF, D), BF),
        pltpu.VMEM((2, 2, 7, HALF, D), BF),
        pltpu.VMEM((8, 8, T), F32),
        pltpu.VMEM((8, 8, T), F32),
        pltpu.VMEM((2, 6, 128, D), BF),
        pltpu.VMEM((2, 6, 128, D), BF),
        pltpu.VMEM((2, 2, 128, D), F32),
        pltpu.VMEM((2, 2, 128, D), F32),
        pltpu.VMEM((2, 128, D), BF),
        pltpu.VMEM((2, 128, D), BF),
        dma((5,)),
        dma((2, 2, 4, 2)), dma((2, 2, 4, 2)),
        dma((8,)), dma((8,)),
        dma((2, 8, 4)), dma((2, 8, 4)),
        dma((2, 8, 4)), dma((2, 8, 4)),
        dma((2, 2, 7)), dma((2, 2, 7)),
        dma((8,)), dma((8,)),
        dma((2, 6)), dma((2, 6)),
        dma((2,)), dma((2,)),
    ]
    mixed, tgrad, gg, gin, gout = pl.pallas_call(
        kernel,
        out_shape=(
            jax.ShapeDtypeStruct((T, D), BF),
            jax.ShapeDtypeStruct((T, D), BF),
            jax.ShapeDtypeStruct((8, T), F32),
            jax.ShapeDtypeStruct((128, D), F32),
            jax.ShapeDtypeStruct((128, D), F32),
        ),
        in_specs=[anyspec] * 5,
        out_specs=(vmem,) * 5,
        scratch_shapes=scratch,
        compiler_params=pltpu.CompilerParams(
            collective_id=0, has_side_effects=True, vmem_limit_bytes=62 * 1024 * 1024
        ),
        cost_estimate=pl.CostEstimate(
            flops=14_000_000_000, bytes_accessed=8_000_000, transcendentals=2_000_000
        ),
    )(tokens, out_grad, meta, w_in, w_out)
    return mixed, tgrad, gg[:4].T, gin[None], gout[None]


def solution(mesh):
    token = P(("rep", "ep"), None)
    weight = P("ep", None, None)
    return jax.shard_map(
        body,
        mesh=mesh,
        in_specs=(token, token, token, token, weight, weight),
        out_specs=(token, token, token, P("ep", "rep", None), P("ep", "rep", None)),
        check_vma=False,
    )
```

```python
import jax
import jax.numpy as jnp
from jax import lax
from jax.experimental import pallas as pl
from jax.experimental.pallas import tpu as pltpu
from jax.sharding import PartitionSpec as P

MESH = pl.DeviceIdType.MESH
BF = jnp.bfloat16
F32 = jnp.float32
NZ, NX = 8, 4
T = 128
HALF = 64
CAP = 32
D = 1024
LOG2_E = 1.4426950408889634
INV_ROOT_TAU = 0.3989422804014327
ERF_P = 0.3275911
ERF_A = (0.254829592, -0.284496736, 1.421413741, -1.453152027, 1.061405429)
ROOT_HALF = 0.7071067811865476

ORDER = (0, 7, 1, 6, 2, 5, 3, 4)
POS = {r: p for p, r in enumerate(ORDER)}
RS_UNITS = (
    ((0, 4), (1, 3), (0, 3), (1, 2), (0, 2), (1, 1), (0, 1)),
    ((1, 4), (0, 5), (1, 5), (0, 6), (1, 6), (0, 7), (1, 7)),
)


def dot(a, b, dims=((1,), (0,))):
    return lax.dot_general(a, b, (dims, ((), ())), preferred_element_type=F32)


def gelu_parts(v):
    bell = jnp.exp2(v * v * (-0.5 * LOG2_E))
    base = 1.0 + jnp.abs(v) * (ERF_P * ROOT_HALF)
    t = pl.reciprocal(base, approx=True)
    t = t * (2.0 - base * t)
    poly = 0.5 * ERF_A[4]
    for a in ERF_A[3::-1]:
        poly = poly * t + 0.5 * a
    tail = poly * t * bell
    return jnp.where(v < 0.0, tail, 1.0 - tail), v * bell * INV_ROOT_TAU


def kernel(
    tok, grd, ids, gates, win, wout,
    mixed_o, tgrad_o, gg_o, gin_o, gout_o,
    ball, metall, sel, selt, gatet, gslot, wi, wo, wit, wot,
    disp, arr, arrt, actt, slope, pre, res, ret,
    mixed_v, tgrad_v, gg_v, gin_v, gout_v, hid,
    rs_send, rs_recv, gg_send, gg_recv,
    wx_send, wx_recv, wx_own, wx_chain, wy_send, wy_recv,
    loc_sem, ag_s, ag_r, meta_s, meta_r, disp_s, disp_r, ret_s, ret_r,
    rs_s, rs_r, gg_s, gg_r, wx_s, wx_r, wy_s, wy_r,
):
    rep = lax.axis_index("rep")
    ep = lax.axis_index("ep")
    x, y_hi = lax.rem(rep, 4), lax.div(rep, 4)
    c, y_lo, z = lax.rem(ep, 2), lax.rem(lax.div(ep, 2), 2), lax.div(ep, 4)
    y = y_hi * 2 + y_lo

    def dev(x_, y_, z_, c_):
        return (lax.div(y_, 2) * 4 + x_, (z_ * 2 + lax.rem(y_, 2)) * 2 + c_)

    def along_z(r):
        return dev(x, y, lax.rem(z + r, 8), c)

    y_up, y_dn = lax.rem(y + 1, 4), lax.rem(y + 3, 4)
    y_to = lax.rem(y + 1 + 2 * c, 4)
    y_from_other = lax.rem(y + 1 + 2 * c, 4)
    y_from_same = lax.rem(y + 3 - 2 * c, 4)
    other = 1 - c
    to_plane = (None, dev(x, y, z, other), dev(x, y_to, z, c), dev(x, y_to, z, other))
    from_plane = (
        None, dev(x, y, z, other), dev(x, y_from_same, z, c), dev(x, y_from_other, z, other),
    )
    x_right, x_left = dev(lax.rem(x + 1, 4), y, z, c), dev(lax.rem(x + 3, 4), y, z, c)
    y_far = dev(x, lax.rem(y + 2, 4), z, c)
    partners = [along_z(r) for r in range(1, 8)]
    partners += [to_plane[1], to_plane[2], to_plane[3], from_plane[2]]
    partners += [x_right, x_left, y_far]

    sent = []

    def rcopy(src, dst, ss, rs, device):
        return pltpu.make_async_remote_copy(
            src_ref=src, dst_ref=dst, send_sem=ss, recv_sem=rs, device_id=device, device_id_type=MESH
        )

    def go(copy):
        copy.start()
        sent.append(copy)

    local = {}

    def lcopy(name, src, dst, i):
        local[name] = pltpu.make_async_copy(src, dst, loc_sem.at[i])
        local[name].start()

    lcopy("x", tok, ball.at[0, 0], 0)
    lcopy("wi", win.at[0], wi, 3)
    lcopy("wo", wout.at[0], wo, 4)
    lcopy("g", grd, ball.at[1, 0], 1)

    def out_copy(name, src, dst, i):
        lcopy(name, src, dst, 5 + i)

    barrier = pltpu.get_barrier_semaphore()
    for p in partners:
        pl.semaphore_signal(barrier, inc=1, device_id=p, device_id_type=MESH)
    pl.semaphore_wait(barrier, len(partners))

    own = (tok, grd)

    def ag(a, d, h, half):
        rows = pl.ds(half * HALF, HALF)
        if h == 1:
            src = own[a].at[rows]
        else:
            src = ball.at[a, 8 - (h - 1) if d == 0 else h - 1, rows]
        dst = ball.at[a, 8 - h if d == 0 else h, rows]
        return rcopy(src, dst, ag_s.at[a, d, h - 1, half], ag_r.at[a, d, h - 1, half],
                     along_z(1 if d == 0 else 7))

    def ag_own(a):
        for i in range(2):
            go(ag(a, 0, 1, i))
            go(ag(a, 1, 1, 1 - i))

    def ag_relay(a, h, i):
        for d in range(2):
            half = d if i == 0 else 1 - d
            ag(a, d, h, half).wait_recv()
            if h < (4 if i == 0 else 3):
                go(ag(a, d, h + 1, half))

    def meta_copy(r):
        return rcopy(metall.at[0], metall.at[8 - r], meta_s.at[8 - r], meta_r.at[8 - r], along_z(r))

    ag_own(0)

    expert = lax.broadcasted_iota(jnp.int32, (32, T), 0)
    named = [jnp.where(ids[k:k + 1, :] == expert, 1.0, 0.0) for k in range(4)]
    earlier = jnp.where(
        lax.broadcasted_iota(jnp.int32, (T, T), 0) < lax.broadcasted_iota(jnp.int32, (T, T), 1), 1.0, 0.0
    ).astype(BF)
    before = dot((named[0] + named[1] + named[2] + named[3]).astype(BF), earlier)
    for k in range(4):
        metall[0, k:k + 1, :] = (
            ids[k:k + 1, :].astype(F32) * CAP + jnp.sum(named[k] * before, axis=0, keepdims=True)
        )
    metall[0, 4:8, :] = gates[...]
    for r in (1, 7, 2, 6, 3, 5, 4):
        go(meta_copy(r))

    row = lax.broadcasted_iota(jnp.int32, (T, T), 0)
    q = lax.div(row, CAP)
    q_c = lax.rem(c + lax.rem(q, 2), 2)
    q_y = lax.rem(y_lo + lax.div(q, 2), 2)
    row_place = (((z * 2 + q_y) * 2 + q_c) * CAP + lax.rem(row, CAP)).astype(F32)

    def onehots(r):
        m = metall[r]
        return [jnp.where(m[k:k + 1, :] == row_place, 1.0, 0.0) for k in range(4)], m

    def build(r):
        if r:
            meta_copy(8 - r).wait_recv()
        hots, m = onehots(r)
        total = hots[0] + hots[1] + hots[2] + hots[3]
        gated = sum(hots[k] * m[4 + k:5 + k, :] for k in range(4))
        sel[r] = total.astype(BF)
        selt[r] = total.T.astype(BF)
        gatet[r] = gated.T.astype(BF)
        gslot[r] = jnp.broadcast_to(jnp.sum(gated, axis=1, keepdims=True), (T, T))

    def disp_copy(a, r, k):
        p = POS[r]
        return rcopy(disp.at[a, p, k - 1], arr.at[a, p, k], disp_s.at[a, p, k], disp_r.at[a, p, k],
                     to_plane[k])

    def dispatch(a, r):
        if r == 0:
            local["x" if a == 0 else "g"].wait()
        rows = dot(sel[r], ball[a, r])
        if a == 1:
            rows = rows * gslot[r][:, 0:1]
        rows = rows.astype(BF)
        p = POS[r]
        for k in (2, 3, 1):
            disp[a, p, k - 1] = rows[k * CAP:(k + 1) * CAP]
            go(disp_copy(a, r, k))
        arr[a, p, 0] = rows[:CAP]

    def ret_copy(a, p, k):
        return rcopy(res.at[a, p, k], ret.at[a, p, k], ret_s.at[a, p, k], ret_r.at[a, p, k],
                     from_plane[k])

    def give_back(a, j):
        for p in (2 * j, 2 * j + 1):
            for k in (2, 3, 1):
                go(ret_copy(a, p, k))
            ret[a, p, 0] = res[a, p, 0]

    awaited = set()

    def await_rows(a, j):
        if (a, j) in awaited:
            return
        awaited.add((a, j))
        for p in (2 * j, 2 * j + 1):
            for k in (1, 2, 3):
                disp_copy(a, ORDER[p], k).wait_recv()

    def turn_weights(n):
        rows = pl.ds(n * 256, 256)
        wit[:, rows] = wi[rows, :].T
        wot[:, rows] = wo[rows, :].T

    def forward_a(j):
        await_rows(0, j)
        rows = arr[0, 2 * j:2 * j + 2].reshape(256, D)
        span = pl.ds(256 * j, 256)
        acts = []
        for n in range(4):
            cols = pl.ds(n * 256, 256)
            v = dot(rows, wi[:, cols])
            below, dense = gelu_parts(v)
            slope[span, cols] = below + dense
            acts.append((v * below).astype(BF))
            actt[cols, span] = acts[-1].T
        hid[...] = jnp.concatenate(acts, axis=1)

    def forward_b(j):
        span = pl.ds(256 * j, 256)
        hidden = hid[...]
        for n in range(4):
            cols = pl.ds(n * 256, 256)
            res[0, 2 * j:2 * j + 2, :, :, cols] = (
                dot(hidden, wo[:, cols]).astype(BF).reshape(2, 4, CAP, 256)
            )
        give_back(0, j)
        arrt[:, span] = arr[0, 2 * j:2 * j + 2].reshape(256, D).T

    def backward_a(j):
        await_rows(1, j)
        rows = arr[1, 2 * j:2 * j + 2].reshape(256, D)
        span = pl.ds(256 * j, 256)
        for n in range(4):
            cols = pl.ds(n * 256, 256)
            pre[span, cols] = (dot(rows, wot[:, cols]) * slope[span, cols]).astype(BF)

    def backward_b(j):
        hidden = pre[pl.ds(256 * j, 256), :]
        for n in range(4):
            cols = pl.ds(n * 256, 256)
            res[1, 2 * j:2 * j + 2, :, :, cols] = (
                dot(hidden, wit[:, cols]).astype(BF).reshape(2, 4, CAP, 256)
            )
        give_back(1, j)

    returned = set()

    def combine(a, r, half):
        p = POS[r]
        if (a, p) not in returned:
            returned.add((a, p))
            for k in (1, 2, 3):
                ret_copy(a, p, k).wait_recv()
        weights = (gatet if a == 0 else selt)[r, half * HALF:(half + 1) * HALF]
        return dot(weights, ret[a, p].reshape(T, D))

    def rs_copy(a, d, i):
        return rcopy(rs_send.at[a, d, i], rs_recv.at[a, d, i], rs_s.at[a, d, i], rs_r.at[a, d, i],
                     along_z(1 if d == 0 else 7))

    def rs(a, i):
        for d in range(2):
            half, r = RS_UNITS[d][i]
            prior = (half, r + 1 if d == 0 else r - 1)
            total = combine(a, r, half)
            if prior in RS_UNITS[d]:
                n = RS_UNITS[d].index(prior)
                rs_copy(a, d, n).wait_recv()
                total = total + rs_recv[a, d, n].astype(F32)
            rs_send[a, d, i] = total.astype(BF)
            go(rs_copy(a, d, i))

    def rs_end(a, out):
        for half in range(2):
            total = combine(a, 0, half)
            for d in range(2):
                n = RS_UNITS[d].index((half, 1 if d == 0 else 7))
                rs_copy(a, d, n).wait_recv()
                total = total + rs_recv[a, d, n].astype(F32)
            out[half * HALF:(half + 1) * HALF, :] = total.astype(BF)

    def gg_copy(r):
        return rcopy(gg_send.at[r], gg_recv.at[r], gg_s.at[r], gg_r.at[r], along_z(r))

    def gate_grad(r):
        m = dot(ret[0, POS[r]].reshape(T, D), ball[1, r], ((1,), (1,)))
        hots, _ = onehots(r)
        out = gg_send if r else gg_recv
        for k in range(4):
            out[r, k:k + 1, :] = jnp.sum(m * hots[k], axis=0, keepdims=True)
        if r:
            out[r, 4:8, :] = jnp.zeros((4, T), F32)
            go(gg_copy(r))

    def wx_copy(w, i):
        return rcopy(wx_send.at[w, i], wx_recv.at[w, i], wx_s.at[w, i], wx_r.at[w, i],
                     x_right if i < 3 else x_left)

    def wgrad(w, dx):
        left = actt if w == 1 else arrt
        dest = lax.rem(x + dx, 4)
        lhs = jnp.concatenate(
            [left[pl.ds(pl.multiple_of((yh * 4 + dest) * 128, 128), 128), :] for yh in range(2)], axis=0
        )
        for n in range(4):
            cols = pl.ds(n * 256, 256)
            right = arr[1, :, :, :, cols].reshape(1024, 256) if w == 1 else pre[:, cols]
            v = dot(lhs, right)
            a, b = v[:128], v[128:]
            if dx == 2:
                wx_send[w, 3, :, cols] = a.astype(BF)
                wx_send[w, 0, :, cols] = b.astype(BF)
            elif dx == 1:
                wx_send[w, 1, :, cols] = a.astype(BF)
                wx_chain[w, 0, :, cols] = b
            elif dx == 3:
                wx_send[w, 4, :, cols] = b.astype(BF)
                wx_chain[w, 1, :, cols] = a
            else:
                wx_own[w, 0, :, cols] = a
                wx_own[w, 1, :, cols] = b
        for i in {2: (3, 0), 1: (1,), 3: (4,), 0: ()}[dx]:
            go(wx_copy(w, i))

    def wchain(w):
        for i, first, n in ((2, 0, 0), (5, 3, 1)):
            wx_copy(w, first).wait_recv()
            wx_send[w, i] = (wx_chain[w, n] + wx_recv[w, first].astype(F32)).astype(BF)
            go(wx_copy(w, i))

    def wy_copy(w):
        return rcopy(wy_send.at[w], wy_recv.at[w], wy_s.at[w], wy_r.at[w], y_far)

    def wsum(w):
        for i in (1, 2, 4, 5):
            wx_copy(w, i).wait_recv()
        wx_own[w, 0] = wx_own[w, 0] + wx_recv[w, 1].astype(F32) + wx_recv[w, 5].astype(F32)
        wx_own[w, 1] = wx_own[w, 1] + wx_recv[w, 2].astype(F32) + wx_recv[w, 4].astype(F32)
        wy_send[w] = wx_own[w, 1 - y_hi].astype(BF)
        go(wy_copy(w))

    def wend(w, out):
        wy_copy(w).wait_recv()
        out[...] = wx_own[w, y_hi] + wy_recv[w].astype(F32)

    build(0)
    dispatch(0, 0)
    local["wi"].wait()
    local["wo"].wait()
    turn_weights(0)
    ag_relay(0, 1, 0)
    build(7)
    build(1)
    turn_weights(1)
    ag_relay(0, 1, 1)
    dispatch(0, 7)
    dispatch(0, 1)
    turn_weights(2)
    ag_relay(0, 2, 0)
    build(6)
    build(2)
    turn_weights(3)
    ag_relay(0, 2, 1)
    dispatch(0, 6)
    dispatch(0, 2)
    forward_a(0)
    ag_relay(0, 3, 0)
    ag_own(1)
    forward_b(0)
    build(5)
    build(3)
    ag_relay(0, 3, 1)
    dispatch(0, 5)
    dispatch(0, 3)
    forward_a(1)
    build(4)
    ag_relay(0, 4, 0)
    dispatch(0, 4)
    forward_b(1)
    dispatch(1, 0)
    ag_relay(1, 1, 0)
    forward_a(2)
    ag_relay(1, 1, 1)
    forward_b(2)
    dispatch(1, 7)
    dispatch(1, 1)
    ag_relay(1, 2, 0)
    forward_a(3)
    ag_relay(1, 2, 1)
    forward_b(3)
    dispatch(1, 6)
    dispatch(1, 2)
    ag_relay(1, 3, 0)
    backward_a(0)
    backward_b(0)
    ag_relay(1, 3, 1)
    dispatch(1, 5)
    dispatch(1, 3)
    backward_a(1)
    backward_b(1)
    ag_relay(1, 4, 0)
    dispatch(1, 4)
    rs(0, 0)
    rs(0, 1)
    backward_a(2)
    backward_b(2)
    rs(0, 2)
    await_rows(1, 3)
    wgrad(1, 2)
    rs(0, 3)
    wgrad(1, 1)
    wgrad(1, 3)
    rs(0, 4)
    backward_a(3)
    backward_b(3)
    rs(0, 5)
    wgrad(0, 2)
    wgrad(1, 0)
    rs(0, 6)
    rs(1, 0)
    rs(1, 1)
    wchain(1)
    wgrad(0, 1)
    wgrad(0, 3)
    rs_end(0, mixed_v)
    out_copy("mixed", mixed_v, mixed_o, 0)
    rs(1, 2)
    wgrad(0, 0)
    for r in (4, 3, 5, 2):
        gate_grad(r)
    rs(1, 3)
    for r in (6, 1, 7, 0):
        gate_grad(r)
    wchain(0)
    wsum(1)
    rs(1, 4)
    rs(1, 5)
    for r in range(1, 8):
        gg_copy(r).wait_recv()
    gg = gg_recv[0, 0:4, :]
    for r in range(1, 8):
        gg = gg + gg_recv[r, 0:4, :]
    gg_v[...] = gg
    out_copy("gg", gg_v, gg_o, 2)
    rs(1, 6)
    wend(1, gout_v)
    out_copy("gout", gout_v, gout_o, 4)
    wsum(0)
    rs_end(1, tgrad_v)
    out_copy("tgrad", tgrad_v, tgrad_o, 1)
    wend(0, gin_v)
    out_copy("gin", gin_v, gin_o, 3)
    for copy in sent:
        copy.wait_send()
    for name in ("mixed", "gg", "gout", "tgrad", "gin"):
        local[name].wait()


def hand_on(*refs):
    ins, outs, vms, sems = refs[:5], refs[5:10], refs[10:15], refs[15]
    loads = [pltpu.make_async_copy(ins[i], vms[i], sems.at[0, i]) for i in range(5)]
    stores = [pltpu.make_async_copy(vms[i], outs[i], sems.at[1, i]) for i in range(5)]
    for load in loads:
        load.start()
    for load, store in zip(loads, stores):
        load.wait()
        store.start()
    for store in stores:
        store.wait()


def body(tokens, expert_ids, gate_probs, out_grad, w_in, w_out):
    anyspec = pl.BlockSpec(memory_space=pl.ANY)
    vmem = pl.BlockSpec(memory_space=pltpu.VMEM)
    dma = pltpu.SemaphoreType.DMA
    scratch = [
        pltpu.VMEM((2, 8, T, D), BF),
        pltpu.VMEM((8, 8, T), F32),
        pltpu.VMEM((8, T, T), BF),
        pltpu.VMEM((8, T, T), BF),
        pltpu.VMEM((8, T, T), BF),
        pltpu.VMEM((8, T, T), F32),
        pltpu.VMEM((D, D), BF),
        pltpu.VMEM((D, D), BF),
        pltpu.VMEM((D, D), BF),
        pltpu.VMEM((D, D), BF),
        pltpu.VMEM((2, 8, 3, CAP, D), BF),
        pltpu.VMEM((2, 8, 4, CAP, D), BF),
        pltpu.VMEM((D, 1024), BF),
        pltpu.VMEM((D, 1024), BF),
        pltpu.VMEM((1024, D), F32),
        pltpu.VMEM((1024, D), BF),
        pltpu.VMEM((2, 8, 4, CAP, D), BF),
        pltpu.VMEM((2, 8, 4, CAP, D), BF),
        pltpu.VMEM((T, D), BF),
        pltpu.VMEM((T, D), BF),
        pltpu.VMEM((4, T), F32),
        pltpu.VMEM((128, D), F32),
        pltpu.VMEM((128, D), F32),
        pltpu.VMEM((256, D), BF),
        pltpu.VMEM((2, 2, 7, HALF, D), BF),
        pltpu.VMEM((2, 2, 7, HALF, D), BF),
        pltpu.VMEM((8, 8, T), F32),
        pltpu.VMEM((8, 8, T), F32),
        pltpu.VMEM((2, 6, 128, D), BF),
        pltpu.VMEM((2, 6, 128, D), BF),
        pltpu.VMEM((2, 2, 128, D), F32),
        pltpu.VMEM((2, 2, 128, D), F32),
        pltpu.VMEM((2, 128, D), BF),
        pltpu.VMEM((2, 128, D), BF),
        dma((10,)),
        dma((2, 2, 4, 2)), dma((2, 2, 4, 2)),
        dma((8,)), dma((8,)),
        dma((2, 8, 4)), dma((2, 8, 4)),
        dma((2, 8, 4)), dma((2, 8, 4)),
        dma((2, 2, 7)), dma((2, 2, 7)),
        dma((8,)), dma((8,)),
        dma((2, 6)), dma((2, 6)),
        dma((2,)), dma((2,)),
    ]
    shapes = (
        jax.ShapeDtypeStruct((T, D), BF),
        jax.ShapeDtypeStruct((T, D), BF),
        jax.ShapeDtypeStruct((4, T), F32),
        jax.ShapeDtypeStruct((128, D), F32),
        jax.ShapeDtypeStruct((128, D), F32),
    )
    results = pl.pallas_call(
        kernel,
        out_shape=shapes,
        in_specs=[anyspec] * 2 + [vmem] * 2 + [anyspec] * 2,
        out_specs=(anyspec,) * 5,
        scratch_shapes=scratch,
        compiler_params=pltpu.CompilerParams(
            collective_id=0, has_side_effects=True, vmem_limit_bytes=63 * 1024 * 1024
        ),
        cost_estimate=pl.CostEstimate(
            flops=14_000_000_000, bytes_accessed=8_000_000, transcendentals=2_000_000
        ),
    )(tokens, out_grad, expert_ids.T, gate_probs.T, w_in, w_out)
    mixed, tgrad, gg, gin, gout = pl.pallas_call(
        hand_on,
        out_shape=shapes,
        in_specs=[anyspec] * 5,
        out_specs=(anyspec,) * 5,
        scratch_shapes=[pltpu.VMEM(shape.shape, shape.dtype) for shape in shapes] + [dma((2, 5))],
    )(*results)
    return mixed, tgrad, gg.T, gin[None], gout[None]


def solution(mesh):
    token = P(("rep", "ep"), None)
    weight = P("ep", None, None)
    return jax.shard_map(
        body,
        mesh=mesh,
        in_specs=(token, token, token, token, weight, weight),
        out_specs=(token, token, token, P("ep", "rep", None), P("ep", "rep", None)),
        check_vma=False,
    )
```

```python
import jax
import jax.numpy as jnp
from jax import lax
from jax.experimental import pallas as pl
from jax.experimental.pallas import tpu as pltpu
from jax.sharding import PartitionSpec as P

MESH = pl.DeviceIdType.MESH
BF = jnp.bfloat16
F32 = jnp.float32
NZ, NX = 8, 4
T = 128
HALF = 64
CAP = 32
D = 1024
LOG2_E = 1.4426950408889634
INV_ROOT_TAU = 0.3989422804014327
ERF_P = 0.3275911
ERF_A = (0.254829592, -0.284496736, 1.421413741, -1.453152027, 1.061405429)
ROOT_HALF = 0.7071067811865476

ORDER = (0, 7, 1, 6, 2, 5, 3, 4)
POS = {r: p for p, r in enumerate(ORDER)}
RS_UNITS = (
    ((0, 4), (1, 3), (0, 3), (1, 2), (0, 2), (1, 1), (0, 1)),
    ((1, 4), (0, 5), (1, 5), (0, 6), (1, 6), (0, 7), (1, 7)),
)


def dot(a, b, dims=((1,), (0,))):
    return lax.dot_general(a, b, (dims, ((), ())), preferred_element_type=F32)


def gelu_parts(v):
    bell = jnp.exp2(v * v * (-0.5 * LOG2_E))
    base = 1.0 + jnp.abs(v) * (ERF_P * ROOT_HALF)
    t = pl.reciprocal(base, approx=True)
    t = t * (2.0 - base * t)
    poly = 0.5 * ERF_A[4]
    for a in ERF_A[3::-1]:
        poly = poly * t + 0.5 * a
    tail = poly * t * bell
    return jnp.where(v < 0.0, tail, 1.0 - tail), v * bell * INV_ROOT_TAU


def kernel(
    tok, grd, ids, gates, win, wout,
    mixed_o, tgrad_o, gg_o, gin_o, gout_o,
    ball, metall, sel, selt, gatet, gslot, wi, wo, wit, wot,
    disp, arr, arrt, actt, slope, pre, res, ret,
    mixed_v, tgrad_v, gg_v, gin_v, gout_v, hid,
    rs_send, rs_recv, gg_send, gg_recv,
    wx_send, wx_recv, wx_own, wx_chain, wy_send, wy_recv,
    loc_sem, ag_s, ag_r, meta_s, meta_r, disp_s, disp_r, ret_s, ret_r,
    rs_s, rs_r, gg_s, gg_r, wx_s, wx_r, wy_s, wy_r,
):
    rep = lax.axis_index("rep")
    ep = lax.axis_index("ep")
    x, y_hi = lax.rem(rep, 4), lax.div(rep, 4)
    c, y_lo, z = lax.rem(ep, 2), lax.rem(lax.div(ep, 2), 2), lax.div(ep, 4)
    y = y_hi * 2 + y_lo

    def dev(x_, y_, z_, c_):
        return (lax.div(y_, 2) * 4 + x_, (z_ * 2 + lax.rem(y_, 2)) * 2 + c_)

    def along_z(r):
        return dev(x, y, lax.rem(z + r, 8), c)

    y_up, y_dn = lax.rem(y + 1, 4), lax.rem(y + 3, 4)
    y_to = lax.rem(y + 1 + 2 * c, 4)
    y_from_other = lax.rem(y + 1 + 2 * c, 4)
    y_from_same = lax.rem(y + 3 - 2 * c, 4)
    other = 1 - c
    to_plane = (None, dev(x, y, z, other), dev(x, y_to, z, c), dev(x, y_to, z, other))
    from_plane = (
        None, dev(x, y, z, other), dev(x, y_from_same, z, c), dev(x, y_from_other, z, other),
    )
    x_right, x_left = dev(lax.rem(x + 1, 4), y, z, c), dev(lax.rem(x + 3, 4), y, z, c)
    y_far = dev(x, lax.rem(y + 2, 4), z, c)
    partners = [along_z(1), along_z(7)]
    partners += [to_plane[1], to_plane[2], to_plane[3], from_plane[2]]
    partners += [x_right, x_left]

    def rcopy(src, dst, ss, rs, device):
        return pltpu.make_async_remote_copy(
            src_ref=src, dst_ref=dst, send_sem=ss, recv_sem=rs, device_id=device, device_id_type=MESH
        )

    def go(copy):
        copy.start()

    local = {}

    def lcopy(name, src, dst, i):
        local[name] = pltpu.make_async_copy(src, dst, loc_sem.at[i])
        local[name].start()

    lcopy("x", tok, ball.at[0, 0], 0)
    lcopy("wi", win.at[0], wi, 3)
    lcopy("wo", wout.at[0], wo, 4)
    lcopy("g", grd, ball.at[1, 0], 1)

    def out_copy(name, src, dst, i):
        lcopy(name, src, dst, 5 + i)

    barrier = pltpu.get_barrier_semaphore()
    for p in partners:
        pl.semaphore_signal(barrier, inc=1, device_id=p, device_id_type=MESH)
    pl.semaphore_wait(barrier, len(partners))

    own = (tok, grd)

    def ag(a, d, h, half):
        rows = pl.ds(half * HALF, HALF)
        if h == 1:
            src = own[a].at[rows]
        else:
            src = ball.at[a, 8 - (h - 1) if d == 0 else h - 1, rows]
        dst = ball.at[a, 8 - h if d == 0 else h, rows]
        return rcopy(src, dst, ag_s.at[0], ag_r.at[a, h - 1, 0 if half == d else 1],
                     along_z(1 if d == 0 else 7))

    def ag_own(a):
        for i in range(2):
            go(ag(a, 0, 1, i))
            go(ag(a, 1, 1, 1 - i))

    def ag_relay(a, h, i):
        rcopy(ball.at[a, 0], ball.at[a, 0], ag_s.at[0], ag_r.at[a, h - 1, i], along_z(1)).wait_recv()
        for d in range(2):
            if h < (4 if i == 0 else 3):
                go(ag(a, d, h + 1, d if i == 0 else 1 - d))

    def meta_copy(d, h):
        src, dst = (8 - (h - 1), 8 - h) if d == 0 else (h - 1, h)
        return rcopy(metall.at[src % 8], metall.at[dst], meta_s.at[0], meta_r.at[d, h - 1],
                     along_z(1 if d == 0 else 7))

    def meta_relay(h):
        for d in range(2 if h < 4 else 1):
            meta_copy(d, h).wait_recv()
            if h < (4 if d == 0 else 3):
                go(meta_copy(d, h + 1))

    ag_own(0)

    expert = lax.broadcasted_iota(jnp.int32, (32, T), 0)
    named = [jnp.where(ids[k:k + 1, :] == expert, 1.0, 0.0) for k in range(4)]
    earlier = jnp.where(
        lax.broadcasted_iota(jnp.int32, (T, T), 0) < lax.broadcasted_iota(jnp.int32, (T, T), 1), 1.0, 0.0
    ).astype(BF)
    before = dot((named[0] + named[1] + named[2] + named[3]).astype(BF), earlier)
    for k in range(4):
        metall[0, k:k + 1, :] = (
            ids[k:k + 1, :].astype(F32) * CAP + jnp.sum(named[k] * before, axis=0, keepdims=True)
        )
    metall[0, 4:8, :] = gates[...]
    for d in range(2):
        go(meta_copy(d, 1))

    row = lax.broadcasted_iota(jnp.int32, (T, T), 0)
    q = lax.div(row, CAP)
    q_c = lax.rem(c + lax.rem(q, 2), 2)
    q_y = lax.rem(y_lo + lax.div(q, 2), 2)
    row_place = (((z * 2 + q_y) * 2 + q_c) * CAP + lax.rem(row, CAP)).astype(F32)

    def onehots(r):
        m = metall[r]
        return [jnp.where(m[k:k + 1, :] == row_place, 1.0, 0.0) for k in range(4)], m

    def build(r):
        hots, m = onehots(r)
        total = hots[0] + hots[1] + hots[2] + hots[3]
        gated = sum(hots[k] * m[4 + k:5 + k, :] for k in range(4))
        sel[r] = total.astype(BF)
        selt[r] = total.T.astype(BF)
        gatet[r] = gated.T.astype(BF)
        gslot[r] = jnp.broadcast_to(jnp.sum(gated, axis=1, keepdims=True), (T, T))

    def disp_copy(a, r, k):
        p = POS[r]
        return rcopy(disp.at[a, p, k - 1], arr.at[a, p, k], disp_s.at[0], disp_r.at[a, p // 2],
                     to_plane[k])

    def dispatch(a, r):
        if r == 0:
            local["x" if a == 0 else "g"].wait()
        rows = dot(sel[r], ball[a, r])
        if a == 1:
            rows = rows * gslot[r][:, 0:1]
        rows = rows.astype(BF)
        p = POS[r]
        for k in (2, 3, 1):
            disp[a, p, k - 1] = rows[k * CAP:(k + 1) * CAP]
            go(disp_copy(a, r, k))
        arr[a, p, 0] = rows[:CAP]

    def ret_copy(a, p, k):
        return rcopy(res.at[a, p, k], ret.at[a, p, k], ret_s.at[0], ret_r.at[a, p],
                     from_plane[k])

    def give_back(a, j):
        for p in (2 * j, 2 * j + 1):
            for k in (2, 3, 1):
                go(ret_copy(a, p, k))
            ret[a, p, 0] = res[a, p, 0]

    awaited = set()

    def await_rows(a, j):
        if (a, j) in awaited:
            return
        awaited.add((a, j))
        two = disp.at[a, 2 * j:2 * j + 2]
        rcopy(two, two, disp_s.at[0], disp_r.at[a, j], to_plane[1]).wait_recv()

    def turn_weights(n):
        rows = pl.ds(n * 256, 256)
        wit[:, rows] = wi[rows, :].T
        wot[:, rows] = wo[rows, :].T

    def forward_a(j):
        await_rows(0, j)
        rows = arr[0, 2 * j:2 * j + 2].reshape(256, D)
        span = pl.ds(256 * j, 256)
        acts = []
        for n in range(4):
            cols = pl.ds(n * 256, 256)
            v = dot(rows, wi[:, cols])
            below, dense = gelu_parts(v)
            slope[span, cols] = below + dense
            acts.append((v * below).astype(BF))
            actt[cols, span] = acts[-1].T
        hid[...] = jnp.concatenate(acts, axis=1)

    def forward_b(j):
        span = pl.ds(256 * j, 256)
        hidden = hid[...]
        for n in range(4):
            cols = pl.ds(n * 256, 256)
            res[0, 2 * j:2 * j + 2, :, :, cols] = (
                dot(hidden, wo[:, cols]).astype(BF).reshape(2, 4, CAP, 256)
            )
        give_back(0, j)
        arrt[:, span] = arr[0, 2 * j:2 * j + 2].reshape(256, D).T

    def backward_a(j):
        await_rows(1, j)
        rows = arr[1, 2 * j:2 * j + 2].reshape(256, D)
        span = pl.ds(256 * j, 256)
        for n in range(4):
            cols = pl.ds(n * 256, 256)
            pre[span, cols] = (dot(rows, wot[:, cols]) * slope[span, cols]).astype(BF)

    def backward_b(j):
        hidden = pre[pl.ds(256 * j, 256), :]
        for n in range(4):
            cols = pl.ds(n * 256, 256)
            res[1, 2 * j:2 * j + 2, :, :, cols] = (
                dot(hidden, wit[:, cols]).astype(BF).reshape(2, 4, CAP, 256)
            )

    returned = set()

    def combine(a, r, half):
        p = POS[r]
        if (a, p) not in returned:
            returned.add((a, p))
            rcopy(disp.at[a, p], disp.at[a, p], ret_s.at[0], ret_r.at[a, p], to_plane[1]).wait_recv()
        weights = (gatet if a == 0 else selt)[r, half * HALF:(half + 1) * HALF]
        return dot(weights, ret[a, p].reshape(T, D))

    def rs_copy(a, d, i):
        return rcopy(rs_send.at[a, d, i], rs_recv.at[a, d, i], rs_s.at[0], rs_r.at[a, i],
                     along_z(1 if d == 0 else 7))

    def rs_await(a, n):
        rcopy(ball.at[a, 0], ball.at[a, 0], rs_s.at[0], rs_r.at[a, n], along_z(1)).wait_recv()

    def rs(a, i):
        if i >= 2:
            rs_await(a, i - 2)
        for d in range(2):
            half, r = RS_UNITS[d][i]
            prior = (half, r + 1 if d == 0 else r - 1)
            total = combine(a, r, half)
            if prior in RS_UNITS[d]:
                total = total + rs_recv[a, d, i - 2].astype(F32)
            rs_send[a, d, i] = total.astype(BF)
            go(rs_copy(a, d, i))

    def rs_end(a, out):
        rs_await(a, 5)
        rs_await(a, 6)
        for half in range(2):
            total = combine(a, 0, half)
            for d in range(2):
                n = RS_UNITS[d].index((half, 1 if d == 0 else 7))
                total = total + rs_recv[a, d, n].astype(F32)
            out[half * HALF:(half + 1) * HALF, :] = total.astype(BF)

    def gg_copy(r):
        return rcopy(gg_send.at[r], gg_recv.at[r], gg_s.at[0], gg_r.at[0], along_z(r))

    def gate_grad(r):
        m = dot(ret[0, POS[r]].reshape(T, D), ball[1, r], ((1,), (1,)))
        hots, _ = onehots(r)
        out = gg_send if r else gg_recv
        for k in range(4):
            out[r, k:k + 1, :] = jnp.sum(m * hots[k], axis=0, keepdims=True)
        if r:
            out[r, 4:8, :] = jnp.zeros((4, T), F32)
            go(gg_copy(r))

    def wx_copy(w, i):
        return rcopy(wx_send.at[w, i], wx_recv.at[w, i], wx_s.at[0], wx_r.at[w, i],
                     x_right if i < 3 else x_left)

    def wgrad(w, dx):
        left = actt if w == 1 else arrt
        dest = lax.rem(x + dx, 4)
        lhs = jnp.concatenate(
            [left[pl.ds(pl.multiple_of((yh * 4 + dest) * 128, 128), 128), :] for yh in (1 - y_hi, y_hi)],
            axis=0,
        )
        for n in range(4):
            cols = pl.ds(n * 256, 256)
            right = arr[1, :, :, :, cols].reshape(1024, 256) if w == 1 else pre[:, cols]
            v = dot(lhs, right)
            far, near = v[:128], v[128:]
            if dx == 2:
                wx_send[w, 0, :, cols] = far.astype(BF)
                wx_send[w, 3, :, cols] = near.astype(BF)
            elif dx == 1:
                wx_send[w, 1, :, cols] = near.astype(BF)
                wx_chain[w, 0, :, cols] = far
            elif dx == 3:
                wx_send[w, 4, :, cols] = far.astype(BF)
                wx_chain[w, 1, :, cols] = near
            else:
                wx_own[w, 0, :, cols] = far
                wx_own[w, 1, :, cols] = near

    def wsend(w, i):
        go(wx_copy(w, i))

    def wchain(w, n):
        i, first = (2, 0) if n == 0 else (5, 3)
        wx_copy(w, first).wait_recv()
        wx_send[w, i] = (wx_chain[w, n] + wx_recv[w, first].astype(F32)).astype(BF)
        go(wx_copy(w, i))

    def wy_copy(w):
        return rcopy(wy_send.at[w], wy_recv.at[w], wy_s.at[0], wy_r.at[w], y_far)

    def wfar(w):
        for i in (2, 4):
            wx_copy(w, i).wait_recv()
        total = wx_own[w, 0] + wx_recv[w, 2].astype(F32) + wx_recv[w, 4].astype(F32)
        wy_send[w] = total.astype(BF)
        go(wy_copy(w))

    def wend(w, out):
        for i in (1, 5):
            wx_copy(w, i).wait_recv()
        total = wx_own[w, 1] + wx_recv[w, 1].astype(F32) + wx_recv[w, 5].astype(F32)
        wy_copy(w).wait_recv()
        out[...] = total + wy_recv[w].astype(F32)

    def backward(j):
        backward_a(j)
        backward_b(j)

    def forward(j):
        forward_a(j)
        forward_b(j)

    build(0)
    dispatch(0, 0)
    local["wi"].wait()
    local["wo"].wait()
    turn_weights(0)
    ag_relay(0, 1, 0)
    meta_relay(1)
    build(7)
    build(1)
    dispatch(1, 0)
    ag_relay(0, 1, 1)
    dispatch(0, 7)
    dispatch(0, 1)
    turn_weights(1)
    ag_relay(0, 2, 0)
    meta_relay(2)
    build(6)
    build(2)
    turn_weights(2)
    ag_relay(0, 2, 1)
    dispatch(0, 6)
    dispatch(0, 2)
    forward_a(0)
    ag_relay(0, 3, 0)
    ag_own(1)
    meta_relay(3)
    build(5)
    build(3)
    forward_b(0)
    ag_relay(0, 3, 1)
    dispatch(0, 5)
    dispatch(0, 3)
    meta_relay(4)
    build(4)
    forward(1)
    ag_relay(0, 4, 0)
    dispatch(0, 4)
    turn_weights(3)
    ag_relay(1, 1, 0)
    forward(2)
    ag_relay(1, 1, 1)
    dispatch(1, 7)
    dispatch(1, 1)
    forward(3)
    ag_relay(1, 2, 0)
    ag_relay(1, 2, 1)
    dispatch(1, 6)
    dispatch(1, 2)
    backward(0)
    ag_relay(1, 3, 0)
    rs(0, 0)
    rs(0, 1)
    backward(1)
    ag_relay(1, 3, 1)
    dispatch(1, 5)
    dispatch(1, 3)
    ag_relay(1, 4, 0)
    dispatch(1, 4)
    give_back(1, 0)
    give_back(1, 1)
    backward(2)
    give_back(1, 2)
    rs(0, 2)
    await_rows(1, 3)
    wgrad(1, 2)
    wsend(1, 0)
    wgrad(1, 3)
    wsend(1, 4)
    rs(0, 3)
    backward(3)
    give_back(1, 3)
    rs(0, 4)
    wgrad(0, 2)
    wsend(0, 0)
    wgrad(0, 3)
    wsend(0, 4)
    wsend(1, 3)
    rs(0, 5)
    wgrad(1, 1)
    wchain(1, 0)
    wsend(0, 3)
    rs(0, 6)
    rs(1, 0)
    rs(1, 1)
    wgrad(0, 1)
    wchain(0, 0)
    wsend(1, 1)
    wsend(0, 1)
    wgrad(1, 0)
    rs_end(0, mixed_v)
    out_copy("mixed", mixed_v, mixed_o, 0)
    wgrad(0, 0)
    for r in (4, 3):
        gate_grad(r)
    rs(1, 2)
    wchain(1, 1)
    wfar(1)
    for r in (5, 2):
        gate_grad(r)
    rs(1, 3)
    wchain(0, 1)
    for r in (6, 1):
        gate_grad(r)
    rs(1, 4)
    wfar(0)
    for r in (7, 0):
        gate_grad(r)
    rs(1, 5)
    rcopy(gg_send.at[1:8], gg_recv.at[1:8], gg_s.at[0], gg_r.at[0], along_z(1)).wait_recv()
    gg = gg_recv[0, 0:4, :]
    for r in range(1, 8):
        gg = gg + gg_recv[r, 0:4, :]
    gg_v[...] = gg
    out_copy("gg", gg_v, gg_o, 2)
    rs(1, 6)
    wend(1, gout_v)
    out_copy("gout", gout_v, gout_o, 4)
    rs_end(1, tgrad_v)
    out_copy("tgrad", tgrad_v, tgrad_o, 1)
    wend(0, gin_v)
    out_copy("gin", gin_v, gin_o, 3)
    for ref, sem in (
        (rs_send, ag_s), (metall.at[1:8], meta_s), (disp, disp_s), (disp, ret_s), (rs_send, rs_s),
        (gg_send.at[1:8], gg_s), (wx_send, wx_s), (wy_send, wy_s),
    ):
        rcopy(ref, ref, sem.at[0], wy_r.at[0], y_far).wait_send()
    for name in ("mixed", "gg", "gout", "tgrad", "gin"):
        local[name].wait()


def hand_on(*refs):
    ins, outs, vms, sems = refs[:5], refs[5:10], refs[10:15], refs[15]
    loads = [pltpu.make_async_copy(ins[i], vms[i], sems.at[0, i]) for i in range(5)]
    stores = [pltpu.make_async_copy(vms[i], outs[i], sems.at[1, i]) for i in range(5)]
    for load in loads:
        load.start()
    for load, store in zip(loads, stores):
        load.wait()
        store.start()
    for store in stores:
        store.wait()


def body(tokens, expert_ids, gate_probs, out_grad, w_in, w_out):
    anyspec = pl.BlockSpec(memory_space=pl.ANY)
    vmem = pl.BlockSpec(memory_space=pltpu.VMEM)
    dma = pltpu.SemaphoreType.DMA
    scratch = [
        pltpu.VMEM((2, 8, T, D), BF),
        pltpu.VMEM((8, 8, T), F32),
        pltpu.VMEM((8, T, T), BF),
        pltpu.VMEM((8, T, T), BF),
        pltpu.VMEM((8, T, T), BF),
        pltpu.VMEM((8, T, T), F32),
        pltpu.VMEM((D, D), BF),
        pltpu.VMEM((D, D), BF),
        pltpu.VMEM((D, D), BF),
        pltpu.VMEM((D, D), BF),
        pltpu.VMEM((2, 8, 3, CAP, D), BF),
        pltpu.VMEM((2, 8, 4, CAP, D), BF),
        pltpu.VMEM((D, 1024), BF),
        pltpu.VMEM((D, 1024), BF),
        pltpu.VMEM((1024, D), F32),
        pltpu.VMEM((1024, D), BF),
        pltpu.VMEM((2, 8, 4, CAP, D), BF),
        pltpu.VMEM((2, 8, 4, CAP, D), BF),
        pltpu.VMEM((T, D), BF),
        pltpu.VMEM((T, D), BF),
        pltpu.VMEM((4, T), F32),
        pltpu.VMEM((128, D), F32),
        pltpu.VMEM((128, D), F32),
        pltpu.VMEM((256, D), BF),
        pltpu.VMEM((2, 2, 7, HALF, D), BF),
        pltpu.VMEM((2, 2, 7, HALF, D), BF),
        pltpu.VMEM((8, 8, T), F32),
        pltpu.VMEM((8, 8, T), F32),
        pltpu.VMEM((2, 6, 128, D), BF),
        pltpu.VMEM((2, 6, 128, D), BF),
        pltpu.VMEM((2, 2, 128, D), F32),
        pltpu.VMEM((2, 2, 128, D), F32),
        pltpu.VMEM((2, 128, D), BF),
        pltpu.VMEM((2, 128, D), BF),
        dma((10,)),
        dma((1,)), dma((2, 4, 2)),
        dma((1,)), dma((2, 4)),
        dma((1,)), dma((2, 4)),
        dma((1,)), dma((2, 8)),
        dma((1,)), dma((2, 7)),
        dma((1,)), dma((1,)),
        dma((1,)), dma((2, 6)),
        dma((1,)), dma((2,)),
    ]
    shapes = (
        jax.ShapeDtypeStruct((T, D), BF),
        jax.ShapeDtypeStruct((T, D), BF),
        jax.ShapeDtypeStruct((4, T), F32),
        jax.ShapeDtypeStruct((128, D), F32),
        jax.ShapeDtypeStruct((128, D), F32),
    )
    results = pl.pallas_call(
        kernel,
        out_shape=shapes,
        in_specs=[anyspec] * 2 + [vmem] * 2 + [anyspec] * 2,
        out_specs=(anyspec,) * 5,
        scratch_shapes=scratch,
        compiler_params=pltpu.CompilerParams(
            collective_id=0, has_side_effects=True, vmem_limit_bytes=63 * 1024 * 1024
        ),
        cost_estimate=pl.CostEstimate(
            flops=14_000_000_000, bytes_accessed=8_000_000, transcendentals=2_000_000
        ),
    )(tokens, out_grad, expert_ids.T, gate_probs.T, w_in, w_out)
    mixed, tgrad, gg, gin, gout = pl.pallas_call(
        hand_on,
        out_shape=shapes,
        in_specs=[anyspec] * 5,
        out_specs=(anyspec,) * 5,
        scratch_shapes=[pltpu.VMEM(shape.shape, shape.dtype) for shape in shapes] + [dma((2, 5))],
    )(*results)
    return mixed, tgrad, gg.T, gin[None], gout[None]


def solution(mesh):
    token = P(("rep", "ep"), None)
    weight = P("ep", None, None)
    return jax.shard_map(
        body,
        mesh=mesh,
        in_specs=(token, token, token, token, weight, weight),
        out_specs=(token, token, token, P("ep", "rep", None), P("ep", "rep", None)),
        check_vma=False,
    )
```

```python
import jax
import jax.numpy as jnp
from jax import lax
from jax.experimental import pallas as pl
from jax.experimental.pallas import tpu as pltpu
from jax.sharding import PartitionSpec as P

MESH = pl.DeviceIdType.MESH
BF = jnp.bfloat16
F32 = jnp.float32
NZ, NX = 8, 4
T = 128
HALF = 64
CAP = 32
D = 1024
LOG2_E = 1.4426950408889634
INV_ROOT_TAU = 0.3989422804014327
ERF_P = 0.3275911
ERF_A = (0.254829592, -0.284496736, 1.421413741, -1.453152027, 1.061405429)
ROOT_HALF = 0.7071067811865476

ORDER = (0, 7, 1, 6, 2, 5, 3, 4)
POS = {r: p for p, r in enumerate(ORDER)}
RS_UNITS = (
    ((0, 4), (1, 3), (0, 3), (1, 2), (0, 2), (1, 1), (0, 1)),
    ((1, 4), (0, 5), (1, 5), (0, 6), (1, 6), (0, 7), (1, 7)),
)


def dot(a, b, dims=((1,), (0,))):
    return lax.dot_general(a, b, (dims, ((), ())), preferred_element_type=F32)


def gelu_parts(v):
    bell = jnp.exp2(v * v * (-0.5 * LOG2_E))
    base = 1.0 + jnp.abs(v) * (ERF_P * ROOT_HALF)
    t = pl.reciprocal(base, approx=True)
    t = t * (2.0 - base * t)
    poly = 0.5 * ERF_A[4]
    for a in ERF_A[3::-1]:
        poly = poly * t + 0.5 * a
    tail = poly * t * bell
    return jnp.where(v < 0.0, tail, 1.0 - tail), v * bell * INV_ROOT_TAU


def kernel(
    tok, grd, ids, gates, win, wout,
    mixed_o, tgrad_o, gg_o, gin_o, gout_o,
    ball, metall, sel, selt, gatet, gslot, wi, wo, wit, wot,
    disp, arr, arrt, actt, slope, pre, res, ret,
    mixed_v, tgrad_v, gg_v, gin_v, gout_v, hid,
    rs_send, rs_recv, gg_send, gg_recv,
    wx_send, wx_recv, wx_own, wx_chain, wy_send, wy_recv,
    loc_sem, ag_s, ag_r, meta_s, meta_r, disp_s, disp_r, ret_s, ret_r,
    rs_s, rs_r, gg_s, gg_r, wx_s, wx_r, wy_s, wy_r,
):
    rep = lax.axis_index("rep")
    ep = lax.axis_index("ep")
    x, y_hi = lax.rem(rep, 4), lax.div(rep, 4)
    c, y_lo, z = lax.rem(ep, 2), lax.rem(lax.div(ep, 2), 2), lax.div(ep, 4)
    y = y_hi * 2 + y_lo

    def dev(x_, y_, z_, c_):
        return (lax.div(y_, 2) * 4 + x_, (z_ * 2 + lax.rem(y_, 2)) * 2 + c_)

    def along_z(r):
        return dev(x, y, lax.rem(z + r, 8), c)

    y_up, y_dn = lax.rem(y + 1, 4), lax.rem(y + 3, 4)
    y_to = lax.rem(y + 1 + 2 * c, 4)
    y_from_other = lax.rem(y + 1 + 2 * c, 4)
    y_from_same = lax.rem(y + 3 - 2 * c, 4)
    other = 1 - c
    to_plane = (None, dev(x, y, z, other), dev(x, y_to, z, c), dev(x, y_to, z, other))
    from_plane = (
        None, dev(x, y, z, other), dev(x, y_from_same, z, c), dev(x, y_from_other, z, other),
    )
    x_right, x_left = dev(lax.rem(x + 1, 4), y, z, c), dev(lax.rem(x + 3, 4), y, z, c)
    y_far = dev(x, lax.rem(y + 2, 4), z, c)
    partners = [along_z(1), along_z(7)]
    partners += [to_plane[1], to_plane[2], to_plane[3], from_plane[2]]
    partners += [x_right, x_left]

    def rcopy(src, dst, ss, rs, device):
        return pltpu.make_async_remote_copy(
            src_ref=src, dst_ref=dst, send_sem=ss, recv_sem=rs, device_id=device, device_id_type=MESH
        )

    def go(copy):
        copy.start()

    local = {}

    def lcopy(name, src, dst, i):
        local[name] = pltpu.make_async_copy(src, dst, loc_sem.at[i])
        local[name].start()

    lcopy("x", tok, ball.at[0, 0], 0)
    lcopy("wi", win.at[0], wi, 3)
    lcopy("wo", wout.at[0], wo, 4)
    lcopy("g", grd, ball.at[1, 0], 1)

    def out_copy(name, src, dst, i):
        lcopy(name, src, dst, 5 + i)

    barrier = pltpu.get_barrier_semaphore()
    for p in partners:
        pl.semaphore_signal(barrier, inc=1, device_id=p, device_id_type=MESH)
    pl.semaphore_wait(barrier, len(partners))

    own = (tok, grd)

    def ag(a, d, h, half):
        rows = pl.ds(half * HALF, HALF)
        if h == 1:
            src = own[a].at[rows]
        else:
            src = ball.at[a, 8 - (h - 1) if d == 0 else h - 1, rows]
        dst = ball.at[a, 8 - h if d == 0 else h, rows]
        return rcopy(src, dst, ag_s.at[0], ag_r.at[a, h - 1, 0 if half == d else 1],
                     along_z(1 if d == 0 else 7))

    def ag_own(a):
        for i in range(2):
            go(ag(a, 0, 1, i))
            go(ag(a, 1, 1, 1 - i))

    def ag_relay(a, h, i):
        rcopy(ball.at[a, 0], ball.at[a, 0], ag_s.at[0], ag_r.at[a, h - 1, i], along_z(1)).wait_recv()
        for d in range(2):
            if h < (4 if i == 0 else 3):
                go(ag(a, d, h + 1, d if i == 0 else 1 - d))

    def meta_copy(d, h):
        src, dst = (8 - (h - 1), 8 - h) if d == 0 else (h - 1, h)
        return rcopy(metall.at[src % 8], metall.at[dst], meta_s.at[0], meta_r.at[d, h - 1],
                     along_z(1 if d == 0 else 7))

    def meta_relay(h):
        for d in range(2 if h < 4 else 1):
            meta_copy(d, h).wait_recv()
            if h < (4 if d == 0 else 3):
                go(meta_copy(d, h + 1))

    ag_own(0)

    expert = lax.broadcasted_iota(jnp.int32, (32, T), 0)
    named = [jnp.where(ids[k:k + 1, :] == expert, 1.0, 0.0) for k in range(4)]
    earlier = jnp.where(
        lax.broadcasted_iota(jnp.int32, (T, T), 0) < lax.broadcasted_iota(jnp.int32, (T, T), 1), 1.0, 0.0
    ).astype(BF)
    before = dot((named[0] + named[1] + named[2] + named[3]).astype(BF), earlier)
    for k in range(4):
        metall[0, k:k + 1, :] = (
            ids[k:k + 1, :].astype(F32) * CAP + jnp.sum(named[k] * before, axis=0, keepdims=True)
        )
    metall[0, 4:8, :] = gates[...]
    for d in range(2):
        go(meta_copy(d, 1))

    row = lax.broadcasted_iota(jnp.int32, (T, T), 0)
    q = lax.div(row, CAP)
    q_c = lax.rem(c + lax.rem(q, 2), 2)
    q_y = lax.rem(y_lo + lax.div(q, 2), 2)
    row_place = (((z * 2 + q_y) * 2 + q_c) * CAP + lax.rem(row, CAP)).astype(F32)

    def onehots(r):
        m = metall[r]
        return [jnp.where(m[k:k + 1, :] == row_place, 1.0, 0.0) for k in range(4)], m

    def build(r):
        hots, m = onehots(r)
        total = hots[0] + hots[1] + hots[2] + hots[3]
        gated = sum(hots[k] * m[4 + k:5 + k, :] for k in range(4))
        sel[r] = total.astype(BF)
        selt[r] = total.T.astype(BF)
        gatet[r] = gated.T.astype(BF)
        gslot[r] = jnp.broadcast_to(jnp.sum(gated, axis=1, keepdims=True), (T, T))

    def disp_copy(a, r, k):
        p = POS[r]
        return rcopy(disp.at[a, p, k - 1], arr.at[a, p, k], disp_s.at[0], disp_r.at[a, p // 2],
                     to_plane[k])

    def dispatch(a, r):
        if r == 0:
            local["x" if a == 0 else "g"].wait()
        rows = dot(sel[r], ball[a, r])
        if a == 1:
            rows = rows * gslot[r][:, 0:1]
        rows = rows.astype(BF)
        p = POS[r]
        for k in (2, 3, 1):
            disp[a, p, k - 1] = rows[k * CAP:(k + 1) * CAP]
            go(disp_copy(a, r, k))
        arr[a, p, 0] = rows[:CAP]

    def ret_copy(a, p, k):
        return rcopy(res.at[a, p, k], ret.at[a, p, k], ret_s.at[0], ret_r.at[a, p],
                     from_plane[k])

    def give_back(a, j):
        for p in (2 * j, 2 * j + 1):
            for k in (2, 3, 1):
                go(ret_copy(a, p, k))
            ret[a, p, 0] = res[a, p, 0]

    awaited = set()

    def await_rows(a, j):
        if (a, j) in awaited:
            return
        awaited.add((a, j))
        two = disp.at[a, 2 * j:2 * j + 2]
        rcopy(two, two, disp_s.at[0], disp_r.at[a, j], to_plane[1]).wait_recv()

    def turn_weights(n):
        rows = pl.ds(n * 256, 256)
        wit[:, rows] = wi[rows, :].T
        wot[:, rows] = wo[rows, :].T

    def forward_a(j):
        await_rows(0, j)
        rows = arr[0, 2 * j:2 * j + 2].reshape(256, D)
        span = pl.ds(256 * j, 256)
        acts = []
        for n in range(4):
            cols = pl.ds(n * 256, 256)
            v = dot(rows, wi[:, cols])
            below, dense = gelu_parts(v)
            slope[span, cols] = below + dense
            acts.append((v * below).astype(BF))
            actt[cols, span] = acts[-1].T
        hid[...] = jnp.concatenate(acts, axis=1)

    def forward_b(j):
        span = pl.ds(256 * j, 256)
        hidden = hid[...]
        for n in range(4):
            cols = pl.ds(n * 256, 256)
            res[0, 2 * j:2 * j + 2, :, :, cols] = (
                dot(hidden, wo[:, cols]).astype(BF).reshape(2, 4, CAP, 256)
            )
        arrt[:, span] = arr[0, 2 * j:2 * j + 2].reshape(256, D).T

    def backward_a(j):
        await_rows(1, j)
        rows = arr[1, 2 * j:2 * j + 2].reshape(256, D)
        span = pl.ds(256 * j, 256)
        for n in range(4):
            cols = pl.ds(n * 256, 256)
            pre[span, cols] = (dot(rows, wot[:, cols]) * slope[span, cols]).astype(BF)

    def backward_b(j):
        hidden = pre[pl.ds(256 * j, 256), :]
        for n in range(4):
            cols = pl.ds(n * 256, 256)
            res[1, 2 * j:2 * j + 2, :, :, cols] = (
                dot(hidden, wit[:, cols]).astype(BF).reshape(2, 4, CAP, 256)
            )

    returned = set()

    def combine(a, r, half):
        p = POS[r]
        if (a, p) not in returned:
            returned.add((a, p))
            rcopy(disp.at[a, p], disp.at[a, p], ret_s.at[0], ret_r.at[a, p], to_plane[1]).wait_recv()
        weights = (gatet if a == 0 else selt)[r, half * HALF:(half + 1) * HALF]
        return dot(weights, ret[a, p].reshape(T, D))

    def rs_copy(a, d, i):
        return rcopy(rs_send.at[a, d, i], rs_recv.at[a, d, i], rs_s.at[0], rs_r.at[a, i],
                     along_z(1 if d == 0 else 7))

    def rs_await(a, n):
        rcopy(ball.at[a, 0], ball.at[a, 0], rs_s.at[0], rs_r.at[a, n], along_z(1)).wait_recv()

    def rs(a, i):
        totals = [combine(a, r, half) for half, r in (RS_UNITS[0][i], RS_UNITS[1][i])]
        if i >= 2:
            rs_await(a, i - 2)
        for d in range(2):
            total = totals[d]
            if i >= 2:
                total = total + rs_recv[a, d, i - 2].astype(F32)
            rs_send[a, d, i] = total.astype(BF)
            go(rs_copy(a, d, i))

    def rs_end(a, out):
        totals = [combine(a, 0, half) for half in range(2)]
        rs_await(a, 5)
        rs_await(a, 6)
        for half in range(2):
            total = totals[half]
            for d in range(2):
                n = RS_UNITS[d].index((half, 1 if d == 0 else 7))
                total = total + rs_recv[a, d, n].astype(F32)
            out[half * HALF:(half + 1) * HALF, :] = total.astype(BF)

    def gg_copy(r):
        return rcopy(gg_send.at[r], gg_recv.at[r], gg_s.at[0], gg_r.at[0], along_z(r))

    def gate_grad(r):
        m = dot(ret[0, POS[r]].reshape(T, D), ball[1, r], ((1,), (1,)))
        hots, _ = onehots(r)
        out = gg_send if r else gg_recv
        for k in range(4):
            out[r, k:k + 1, :] = jnp.sum(m * hots[k], axis=0, keepdims=True)
        if r:
            out[r, 4:8, :] = jnp.zeros((4, T), F32)
            go(gg_copy(r))

    def wx_copy(w, i):
        return rcopy(wx_send.at[w, i], wx_recv.at[w, i], wx_s.at[0], wx_r.at[w, i],
                     x_right if i < 3 else x_left)

    def wgrad(w, dx):
        left = actt if w == 1 else arrt
        dest = lax.rem(x + dx, 4)
        lhs = jnp.concatenate(
            [left[pl.ds(pl.multiple_of((yh * 4 + dest) * 128, 128), 128), :] for yh in (1 - y_hi, y_hi)],
            axis=0,
        )
        for n in range(4):
            cols = pl.ds(n * 256, 256)
            right = arr[1, :, :, :, cols].reshape(1024, 256) if w == 1 else pre[:, cols]
            v = dot(lhs, right)
            far, near = v[:128], v[128:]
            if dx == 2:
                wx_send[w, 0, :, cols] = far.astype(BF)
                wx_send[w, 3, :, cols] = near.astype(BF)
            elif dx == 1:
                wx_send[w, 1, :, cols] = near.astype(BF)
                wx_chain[w, 0, :, cols] = far
            elif dx == 3:
                wx_send[w, 4, :, cols] = far.astype(BF)
                wx_chain[w, 1, :, cols] = near
            else:
                wx_own[w, 0, :, cols] = far
                wx_own[w, 1, :, cols] = near

    def wsend(w, i):
        go(wx_copy(w, i))

    def wchain(w, n):
        i, first = (2, 0) if n == 0 else (5, 3)
        wx_copy(w, first).wait_recv()
        wx_send[w, i] = (wx_chain[w, n] + wx_recv[w, first].astype(F32)).astype(BF)
        go(wx_copy(w, i))

    def wy_copy(w):
        return rcopy(wy_send.at[w], wy_recv.at[w], wy_s.at[0], wy_r.at[w], y_far)

    def wfar(w):
        for i in (2, 4):
            wx_copy(w, i).wait_recv()
        total = wx_own[w, 0] + wx_recv[w, 2].astype(F32) + wx_recv[w, 4].astype(F32)
        wy_send[w] = total.astype(BF)
        go(wy_copy(w))

    def wend(w, out):
        wy_copy(w).wait_recv()
        wx_copy(w, 1).wait_recv()
        total = wx_own[w, 1] + wx_recv[w, 1].astype(F32) + wy_recv[w].astype(F32)
        wx_copy(w, 5).wait_recv()
        out[...] = total + wx_recv[w, 5].astype(F32)

    def backward(j):
        backward_a(j)
        backward_b(j)

    build(0)
    dispatch(0, 0)
    local["wi"].wait()
    local["wo"].wait()
    turn_weights(0)
    ag_relay(0, 1, 0)
    meta_relay(1)
    build(7)
    build(1)
    turn_weights(1)
    ag_relay(0, 1, 1)
    dispatch(0, 7)
    dispatch(0, 1)
    ag_relay(0, 2, 0)
    meta_relay(2)
    build(6)
    build(2)
    ag_relay(0, 2, 1)
    dispatch(0, 6)
    dispatch(0, 2)
    forward_a(0)
    ag_relay(0, 3, 0)
    ag_own(1)
    meta_relay(3)
    build(5)
    build(3)
    forward_b(0)
    give_back(0, 0)
    ag_relay(0, 3, 1)
    dispatch(0, 5)
    dispatch(0, 3)
    forward_a(1)
    meta_relay(4)
    build(4)
    ag_relay(0, 4, 0)
    dispatch(0, 4)
    forward_b(1)
    give_back(0, 1)
    ag_relay(1, 1, 0)
    forward_a(2)
    forward_b(2)
    give_back(0, 2)
    ag_relay(1, 1, 1)
    forward_a(3)
    forward_b(3)
    give_back(0, 3)
    dispatch(1, 0)
    dispatch(1, 7)
    dispatch(1, 1)
    ag_relay(1, 2, 0)
    turn_weights(2)
    ag_relay(1, 2, 1)
    dispatch(1, 6)
    dispatch(1, 2)
    turn_weights(3)
    ag_relay(1, 3, 0)
    ag_relay(1, 3, 1)
    dispatch(1, 5)
    dispatch(1, 3)
    rs(0, 0)
    rs(0, 1)
    backward(0)
    ag_relay(1, 4, 0)
    dispatch(1, 4)
    give_back(1, 0)
    backward(1)
    give_back(1, 1)
    rs(0, 2)
    await_rows(1, 2)
    await_rows(1, 3)
    wgrad(1, 2)
    wsend(1, 0)
    wgrad(1, 3)
    wsend(1, 4)
    rs(0, 3)
    backward(2)
    give_back(1, 2)
    backward(3)
    give_back(1, 3)
    rs(0, 4)
    wgrad(0, 2)
    wsend(0, 0)
    wgrad(0, 3)
    wsend(0, 4)
    wsend(1, 3)
    wsend(0, 3)
    rs(0, 5)
    wgrad(1, 1)
    wchain(1, 0)
    rs(0, 6)
    wgrad(0, 1)
    rs(1, 0)
    rs(1, 1)
    wgrad(1, 0)
    wchain(0, 0)
    wsend(1, 1)
    wsend(0, 1)
    rs_end(0, mixed_v)
    out_copy("mixed", mixed_v, mixed_o, 0)
    wgrad(0, 0)
    for r in (4, 3):
        gate_grad(r)
    rs(1, 2)
    wchain(1, 1)
    for r in (5, 2):
        gate_grad(r)
    rs(1, 3)
    wfar(1)
    for r in (6, 1):
        gate_grad(r)
    rs(1, 4)
    for r in (7, 0):
        gate_grad(r)
    wchain(0, 1)
    wfar(0)
    rs(1, 5)
    rs(1, 6)
    rcopy(gg_send.at[1:8], gg_recv.at[1:8], gg_s.at[0], gg_r.at[0], along_z(1)).wait_recv()
    gg = gg_recv[0, 0:4, :]
    for r in range(1, 8):
        gg = gg + gg_recv[r, 0:4, :]
    gg_v[...] = gg
    out_copy("gg", gg_v, gg_o, 2)
    wend(1, gout_v)
    out_copy("gout", gout_v, gout_o, 4)
    rs_end(1, tgrad_v)
    out_copy("tgrad", tgrad_v, tgrad_o, 1)
    wend(0, gin_v)
    out_copy("gin", gin_v, gin_o, 3)
    for ref, sem in (
        (rs_send, ag_s), (metall.at[1:8], meta_s), (disp, disp_s), (disp, ret_s), (rs_send, rs_s),
        (gg_send.at[1:8], gg_s), (wx_send, wx_s), (wy_send, wy_s),
    ):
        rcopy(ref, ref, sem.at[0], wy_r.at[0], y_far).wait_send()
    for name in ("mixed", "gg", "gout", "tgrad", "gin"):
        local[name].wait()


def hand_on(*refs):
    ins, outs, vms, sems = refs[:5], refs[5:10], refs[10:15], refs[15]
    loads = [pltpu.make_async_copy(ins[i], vms[i], sems.at[0, i]) for i in range(5)]
    stores = [pltpu.make_async_copy(vms[i], outs[i], sems.at[1, i]) for i in range(5)]
    for load in loads:
        load.start()
    for load, store in zip(loads, stores):
        load.wait()
        store.start()
    for store in stores:
        store.wait()


def body(tokens, expert_ids, gate_probs, out_grad, w_in, w_out):
    anyspec = pl.BlockSpec(memory_space=pl.ANY)
    vmem = pl.BlockSpec(memory_space=pltpu.VMEM)
    dma = pltpu.SemaphoreType.DMA
    scratch = [
        pltpu.VMEM((2, 8, T, D), BF),
        pltpu.VMEM((8, 8, T), F32),
        pltpu.VMEM((8, T, T), BF),
        pltpu.VMEM((8, T, T), BF),
        pltpu.VMEM((8, T, T), BF),
        pltpu.VMEM((8, T, T), F32),
        pltpu.VMEM((D, D), BF),
        pltpu.VMEM((D, D), BF),
        pltpu.VMEM((D, D), BF),
        pltpu.VMEM((D, D), BF),
        pltpu.VMEM((2, 8, 3, CAP, D), BF),
        pltpu.VMEM((2, 8, 4, CAP, D), BF),
        pltpu.VMEM((D, 1024), BF),
        pltpu.VMEM((D, 1024), BF),
        pltpu.VMEM((1024, D), F32),
        pltpu.VMEM((1024, D), BF),
        pltpu.VMEM((2, 8, 4, CAP, D), BF),
        pltpu.VMEM((2, 8, 4, CAP, D), BF),
        pltpu.VMEM((T, D), BF),
        pltpu.VMEM((T, D), BF),
        pltpu.VMEM((4, T), F32),
        pltpu.VMEM((128, D), F32),
        pltpu.VMEM((128, D), F32),
        pltpu.VMEM((256, D), BF),
        pltpu.VMEM((2, 2, 7, HALF, D), BF),
        pltpu.VMEM((2, 2, 7, HALF, D), BF),
        pltpu.VMEM((8, 8, T), F32),
        pltpu.VMEM((8, 8, T), F32),
        pltpu.VMEM((2, 6, 128, D), BF),
        pltpu.VMEM((2, 6, 128, D), BF),
        pltpu.VMEM((2, 2, 128, D), F32),
        pltpu.VMEM((2, 2, 128, D), F32),
        pltpu.VMEM((2, 128, D), BF),
        pltpu.VMEM((2, 128, D), BF),
        dma((10,)),
        dma((1,)), dma((2, 4, 2)),
        dma((1,)), dma((2, 4)),
        dma((1,)), dma((2, 4)),
        dma((1,)), dma((2, 8)),
        dma((1,)), dma((2, 7)),
        dma((1,)), dma((1,)),
        dma((1,)), dma((2, 6)),
        dma((1,)), dma((2,)),
    ]
    shapes = (
        jax.ShapeDtypeStruct((T, D), BF),
        jax.ShapeDtypeStruct((T, D), BF),
        jax.ShapeDtypeStruct((4, T), F32),
        jax.ShapeDtypeStruct((128, D), F32),
        jax.ShapeDtypeStruct((128, D), F32),
    )
    results = pl.pallas_call(
        kernel,
        out_shape=shapes,
        in_specs=[anyspec] * 2 + [vmem] * 2 + [anyspec] * 2,
        out_specs=(anyspec,) * 5,
        scratch_shapes=scratch,
        compiler_params=pltpu.CompilerParams(
            collective_id=0, has_side_effects=True, vmem_limit_bytes=63 * 1024 * 1024
        ),
        cost_estimate=pl.CostEstimate(
            flops=14_000_000_000, bytes_accessed=8_000_000, transcendentals=2_000_000
        ),
    )(tokens, out_grad, expert_ids.T, gate_probs.T, w_in, w_out)
    mixed, tgrad, gg, gin, gout = pl.pallas_call(
        hand_on,
        out_shape=shapes,
        in_specs=[anyspec] * 5,
        out_specs=(anyspec,) * 5,
        scratch_shapes=[pltpu.VMEM(shape.shape, shape.dtype) for shape in shapes] + [dma((2, 5))],
    )(*results)
    return mixed, tgrad, gg.T, gin[None], gout[None]


def solution(mesh):
    token = P(("rep", "ep"), None)
    weight = P("ep", None, None)
    return jax.shard_map(
        body,
        mesh=mesh,
        in_specs=(token, token, token, token, weight, weight),
        out_specs=(token, token, token, P("ep", "rep", None), P("ep", "rep", None)),
        check_vma=False,
    )
```

```python
import jax
import jax.numpy as jnp
from jax import lax
from jax.experimental import pallas as pl
from jax.experimental.pallas import tpu as pltpu
from jax.sharding import PartitionSpec as P

MESH = pl.DeviceIdType.MESH
BF = jnp.bfloat16
F32 = jnp.float32
NZ, NX = 8, 4
T = 128
HALF = 64
CAP = 32
D = 1024
LOG2_E = 1.4426950408889634
INV_ROOT_TAU = 0.3989422804014327
ERF_P = 0.3275911
ERF_A = (0.254829592, -0.284496736, 1.421413741, -1.453152027, 1.061405429)
ROOT_HALF = 0.7071067811865476

ORDER = (0, 7, 1, 6, 2, 5, 3, 4)
POS = {r: p for p, r in enumerate(ORDER)}
RS_UNITS = (
    ((0, 4), (1, 3), (0, 3), (1, 2), (0, 2), (1, 1), (0, 1)),
    ((1, 4), (0, 5), (1, 5), (0, 6), (1, 6), (0, 7), (1, 7)),
)


def dot(a, b, dims=((1,), (0,))):
    return lax.dot_general(a, b, (dims, ((), ())), preferred_element_type=F32)


def gelu_parts(v):
    bell = jnp.exp2(v * v * (-0.5 * LOG2_E))
    base = 1.0 + jnp.abs(v) * (ERF_P * ROOT_HALF)
    t = pl.reciprocal(base, approx=True)
    t = t * (2.0 - base * t)
    poly = 0.5 * ERF_A[4]
    for a in ERF_A[3::-1]:
        poly = poly * t + 0.5 * a
    tail = poly * t * bell
    return jnp.where(v < 0.0, tail, 1.0 - tail), v * bell * INV_ROOT_TAU


def kernel(
    tok, grd, ids_o, gates_o, win, wout,
    mixed_o, tgrad_o, gg_o, gin_o, gout_o,
    ids, gates, ball, metall, sel, selt, gatet, gslot, wi, wo, wit, wot,
    disp, arr, arrt, actt, slope, pre, res, ret,
    mixed_v, tgrad_v, gg_v, gin_v, gout_v, hid,
    rs_send, rs_recv, gg_send, gg_recv,
    wx_send, wx_recv, wx_own, wx_chain, wy_send, wy_recv,
    loc_sem, ag_s, ag_r, meta_s, meta_r, disp_s, disp_r, ret_s, ret_r,
    rs_s, rs_r, gg_s, gg_r, wx_s, wx_r, wy_s, wy_r,
):
    rep = lax.axis_index("rep")
    ep = lax.axis_index("ep")
    x, y_hi = lax.rem(rep, 4), lax.div(rep, 4)
    c, y_lo, z = lax.rem(ep, 2), lax.rem(lax.div(ep, 2), 2), lax.div(ep, 4)
    y = y_hi * 2 + y_lo

    def dev(x_, y_, z_, c_):
        return (lax.div(y_, 2) * 4 + x_, (z_ * 2 + lax.rem(y_, 2)) * 2 + c_)

    def along_z(r):
        return dev(x, y, lax.rem(z + r, 8), c)

    y_up, y_dn = lax.rem(y + 1, 4), lax.rem(y + 3, 4)
    y_to = lax.rem(y + 1 + 2 * c, 4)
    y_from_other = lax.rem(y + 1 + 2 * c, 4)
    y_from_same = lax.rem(y + 3 - 2 * c, 4)
    other = 1 - c
    to_plane = (None, dev(x, y, z, other), dev(x, y_to, z, c), dev(x, y_to, z, other))
    from_plane = (
        None, dev(x, y, z, other), dev(x, y_from_same, z, c), dev(x, y_from_other, z, other),
    )
    x_right, x_left = dev(lax.rem(x + 1, 4), y, z, c), dev(lax.rem(x + 3, 4), y, z, c)
    y_far = dev(x, lax.rem(y + 2, 4), z, c)
    partners = [along_z(1), along_z(7)]
    partners += [to_plane[1], to_plane[2], to_plane[3], from_plane[2]]
    partners += [x_right, x_left]

    def rcopy(src, dst, ss, rs, device):
        return pltpu.make_async_remote_copy(
            src_ref=src, dst_ref=dst, send_sem=ss, recv_sem=rs, device_id=device, device_id_type=MESH
        )

    def go(copy):
        copy.start()

    local = {}

    def lcopy(name, src, dst, i):
        local[name] = pltpu.make_async_copy(src, dst, loc_sem.at[i])
        local[name].start()


    def out_copy(name, src, dst, i):
        lcopy(name, src, dst, 5 + i)

    barrier = pltpu.get_barrier_semaphore()
    for p in partners:
        pl.semaphore_signal(barrier, inc=1, device_id=p, device_id_type=MESH)
    lcopy("ids", ids_o, ids, 2)
    lcopy("gates", gates_o, gates, 10)
    lcopy("x", tok, ball.at[0, 0], 0)
    lcopy("wi", win.at[0], wi, 3)
    lcopy("wo", wout.at[0], wo, 4)
    lcopy("g", grd, ball.at[1, 0], 1)
    pl.semaphore_wait(barrier, len(partners))

    own = (tok, grd)

    def ag(a, d, h, half):
        rows = pl.ds(half * HALF, HALF)
        if h == 1:
            src = own[a].at[rows]
        else:
            src = ball.at[a, 8 - (h - 1) if d == 0 else h - 1, rows]
        dst = ball.at[a, 8 - h if d == 0 else h, rows]
        return rcopy(src, dst, ag_s.at[0], ag_r.at[a, h - 1, 0 if half == d else 1],
                     along_z(1 if d == 0 else 7))

    def ag_own(a):
        for i in range(2):
            go(ag(a, 0, 1, i))
            go(ag(a, 1, 1, 1 - i))

    def ag_relay(a, h, i):
        rcopy(ball.at[a, 0], ball.at[a, 0], ag_s.at[0], ag_r.at[a, h - 1, i], along_z(1)).wait_recv()
        for d in range(2):
            if h < (4 if i == 0 else 3):
                go(ag(a, d, h + 1, d if i == 0 else 1 - d))

    def meta_copy(d, h):
        src, dst = (8 - (h - 1), 8 - h) if d == 0 else (h - 1, h)
        return rcopy(metall.at[src % 8], metall.at[dst], meta_s.at[0], meta_r.at[d, h - 1],
                     along_z(1 if d == 0 else 7))

    def meta_relay(h):
        for d in range(2 if h < 4 else 1):
            meta_copy(d, h).wait_recv()
            if h < (4 if d == 0 else 3):
                go(meta_copy(d, h + 1))

    ag_own(0)

    local["ids"].wait()
    local["gates"].wait()
    expert = lax.broadcasted_iota(jnp.int32, (32, T), 0)
    named = [jnp.where(ids[k:k + 1, :] == expert, 1.0, 0.0) for k in range(4)]
    earlier = jnp.where(
        lax.broadcasted_iota(jnp.int32, (T, T), 0) < lax.broadcasted_iota(jnp.int32, (T, T), 1), 1.0, 0.0
    ).astype(BF)
    before = dot((named[0] + named[1] + named[2] + named[3]).astype(BF), earlier)
    for k in range(4):
        metall[0, k:k + 1, :] = (
            ids[k:k + 1, :].astype(F32) * CAP + jnp.sum(named[k] * before, axis=0, keepdims=True)
        )
    metall[0, 4:8, :] = gates[...]
    for d in range(2):
        go(meta_copy(d, 1))

    row = lax.broadcasted_iota(jnp.int32, (T, T), 0)
    q = lax.div(row, CAP)
    q_c = lax.rem(c + lax.rem(q, 2), 2)
    q_y = lax.rem(y_lo + lax.div(q, 2), 2)
    row_place = (((z * 2 + q_y) * 2 + q_c) * CAP + lax.rem(row, CAP)).astype(F32)

    def onehots(r):
        m = metall[r]
        return [jnp.where(m[k:k + 1, :] == row_place, 1.0, 0.0) for k in range(4)], m

    def build(r):
        hots, m = onehots(r)
        total = hots[0] + hots[1] + hots[2] + hots[3]
        gated = sum(hots[k] * m[4 + k:5 + k, :] for k in range(4))
        sel[r] = total.astype(BF)
        selt[r] = total.T.astype(BF)
        gatet[r] = gated.T.astype(BF)
        gslot[r] = jnp.broadcast_to(jnp.sum(gated, axis=1, keepdims=True), (T, T))

    def disp_copy(a, r, k):
        p = POS[r]
        return rcopy(disp.at[a, p, k - 1], arr.at[a, p, k], disp_s.at[0], disp_r.at[a, p // 2],
                     to_plane[k])

    def dispatch(a, r):
        if r == 0:
            local["x" if a == 0 else "g"].wait()
        rows = dot(sel[r], ball[a, r])
        if a == 1:
            rows = rows * gslot[r][:, 0:1]
        rows = rows.astype(BF)
        p = POS[r]
        for k in (2, 3, 1):
            disp[a, p, k - 1] = rows[k * CAP:(k + 1) * CAP]
            go(disp_copy(a, r, k))
        arr[a, p, 0] = rows[:CAP]

    def ret_copy(a, p, k):
        return rcopy(res.at[a, p, k], ret.at[a, p, k], ret_s.at[0], ret_r.at[a, p],
                     from_plane[k])

    def give_back(a, j):
        for p in (2 * j, 2 * j + 1):
            for k in (2, 3, 1):
                go(ret_copy(a, p, k))
            ret[a, p, 0] = res[a, p, 0]

    awaited = set()

    def await_rows(a, j):
        if (a, j) in awaited:
            return
        awaited.add((a, j))
        two = disp.at[a, 2 * j:2 * j + 2]
        rcopy(two, two, disp_s.at[0], disp_r.at[a, j], to_plane[1]).wait_recv()

    def turn_weights(n):
        rows = pl.ds(n * 256, 256)
        wit[:, rows] = wi[rows, :].T
        wot[:, rows] = wo[rows, :].T

    def forward_a(j):
        await_rows(0, j)
        rows = arr[0, 2 * j:2 * j + 2].reshape(256, D)
        span = pl.ds(256 * j, 256)
        acts = []
        for n in range(4):
            cols = pl.ds(n * 256, 256)
            v = dot(rows, wi[:, cols])
            below, dense = gelu_parts(v)
            slope[span, cols] = below + dense
            acts.append((v * below).astype(BF))
            actt[cols, span] = acts[-1].T
        hid[...] = jnp.concatenate(acts, axis=1)

    def forward_b(j):
        span = pl.ds(256 * j, 256)
        hidden = hid[...]
        for n in range(4):
            cols = pl.ds(n * 256, 256)
            res[0, 2 * j:2 * j + 2, :, :, cols] = (
                dot(hidden, wo[:, cols]).astype(BF).reshape(2, 4, CAP, 256)
            )
        arrt[:, span] = arr[0, 2 * j:2 * j + 2].reshape(256, D).T

    def backward_a(j):
        await_rows(1, j)
        rows = arr[1, 2 * j:2 * j + 2].reshape(256, D)
        span = pl.ds(256 * j, 256)
        for n in range(4):
            cols = pl.ds(n * 256, 256)
            pre[span, cols] = (dot(rows, wot[:, cols]) * slope[span, cols]).astype(BF)

    def backward_b(j):
        hidden = pre[pl.ds(256 * j, 256), :]
        for n in range(4):
            cols = pl.ds(n * 256, 256)
            res[1, 2 * j:2 * j + 2, :, :, cols] = (
                dot(hidden, wit[:, cols]).astype(BF).reshape(2, 4, CAP, 256)
            )

    returned = set()

    def combine(a, r, half):
        p = POS[r]
        if (a, p) not in returned:
            returned.add((a, p))
            rcopy(disp.at[a, p], disp.at[a, p], ret_s.at[0], ret_r.at[a, p], to_plane[1]).wait_recv()
        weights = (gatet if a == 0 else selt)[r, half * HALF:(half + 1) * HALF]
        return dot(weights, ret[a, p].reshape(T, D))

    def rs_copy(a, d, i):
        return rcopy(rs_send.at[a, d, i], rs_recv.at[a, d, i], rs_s.at[0], rs_r.at[a, i],
                     along_z(1 if d == 0 else 7))

    def rs_await(a, n):
        rcopy(ball.at[a, 0], ball.at[a, 0], rs_s.at[0], rs_r.at[a, n], along_z(1)).wait_recv()

    def rs(a, i):
        totals = [combine(a, r, half) for half, r in (RS_UNITS[0][i], RS_UNITS[1][i])]
        if i >= 2:
            rs_await(a, i - 2)
        for d in range(2):
            total = totals[d]
            if i >= 2:
                total = total + rs_recv[a, d, i - 2].astype(F32)
            rs_send[a, d, i] = total.astype(BF)
            go(rs_copy(a, d, i))

    def rs_end(a, out):
        totals = [combine(a, 0, half) for half in range(2)]
        rs_await(a, 5)
        rs_await(a, 6)
        for half in range(2):
            total = totals[half]
            for d in range(2):
                n = RS_UNITS[d].index((half, 1 if d == 0 else 7))
                total = total + rs_recv[a, d, n].astype(F32)
            out[half * HALF:(half + 1) * HALF, :] = total.astype(BF)

    def gg_copy(r):
        return rcopy(gg_send.at[r], gg_recv.at[r], gg_s.at[0], gg_r.at[0], along_z(r))

    def gate_grad(r):
        m = dot(ret[0, POS[r]].reshape(T, D), ball[1, r], ((1,), (1,)))
        hots, _ = onehots(r)
        out = gg_send if r else gg_recv
        for k in range(4):
            out[r, k:k + 1, :] = jnp.sum(m * hots[k], axis=0, keepdims=True)
        if r:
            out[r, 4:8, :] = jnp.zeros((4, T), F32)
            go(gg_copy(r))

    def wx_copy(w, i):
        return rcopy(wx_send.at[w, i], wx_recv.at[w, i], wx_s.at[0], wx_r.at[w, i],
                     x_right if i < 3 else x_left)

    def wgrad(w, dx):
        left = actt if w == 1 else arrt
        dest = lax.rem(x + dx, 4)
        lhs = jnp.concatenate(
            [left[pl.ds(pl.multiple_of((yh * 4 + dest) * 128, 128), 128), :] for yh in (1 - y_hi, y_hi)],
            axis=0,
        )
        for n in range(4):
            cols = pl.ds(n * 256, 256)
            right = arr[1, :, :, :, cols].reshape(1024, 256) if w == 1 else pre[:, cols]
            v = dot(lhs, right)
            far, near = v[:128], v[128:]
            if dx == 2:
                wx_send[w, 0, :, cols] = far.astype(BF)
                wx_send[w, 3, :, cols] = near.astype(BF)
            elif dx == 1:
                wx_send[w, 1, :, cols] = near.astype(BF)
                wx_chain[w, 0, :, cols] = far
            elif dx == 3:
                wx_send[w, 4, :, cols] = far.astype(BF)
                wx_chain[w, 1, :, cols] = near
            else:
                wx_own[w, 0, :, cols] = far
                wx_own[w, 1, :, cols] = near

    def wsend(w, i):
        go(wx_copy(w, i))

    def wchain(w, n):
        i, first = (2, 0) if n == 0 else (5, 3)
        wx_copy(w, first).wait_recv()
        wx_send[w, i] = (wx_chain[w, n] + wx_recv[w, first].astype(F32)).astype(BF)
        go(wx_copy(w, i))

    def wy_copy(w):
        return rcopy(wy_send.at[w], wy_recv.at[w], wy_s.at[0], wy_r.at[w], y_far)

    def wfar(w):
        for i in (2, 4):
            wx_copy(w, i).wait_recv()
        total = wx_own[w, 0] + wx_recv[w, 2].astype(F32) + wx_recv[w, 4].astype(F32)
        wy_send[w] = total.astype(BF)
        go(wy_copy(w))

    def wend(w, out):
        wy_copy(w).wait_recv()
        wx_copy(w, 1).wait_recv()
        total = wx_own[w, 1] + wx_recv[w, 1].astype(F32) + wy_recv[w].astype(F32)
        wx_copy(w, 5).wait_recv()
        out[...] = total + wx_recv[w, 5].astype(F32)

    def backward(j):
        backward_a(j)
        backward_b(j)

    build(0)
    dispatch(0, 0)
    local["wi"].wait()
    local["wo"].wait()
    turn_weights(0)
    ag_relay(0, 1, 0)
    meta_relay(1)
    build(7)
    build(1)
    turn_weights(1)
    ag_relay(0, 1, 1)
    dispatch(0, 7)
    dispatch(0, 1)
    ag_relay(0, 2, 0)
    meta_relay(2)
    build(6)
    build(2)
    ag_relay(0, 2, 1)
    dispatch(0, 6)
    dispatch(0, 2)
    forward_a(0)
    ag_relay(0, 3, 0)
    ag_own(1)
    meta_relay(3)
    build(5)
    build(3)
    forward_b(0)
    give_back(0, 0)
    ag_relay(0, 3, 1)
    dispatch(0, 5)
    dispatch(0, 3)
    forward_a(1)
    meta_relay(4)
    build(4)
    ag_relay(0, 4, 0)
    dispatch(0, 4)
    forward_b(1)
    give_back(0, 1)
    ag_relay(1, 1, 0)
    forward_a(2)
    forward_b(2)
    give_back(0, 2)
    ag_relay(1, 1, 1)
    forward_a(3)
    forward_b(3)
    give_back(0, 3)
    dispatch(1, 0)
    dispatch(1, 7)
    dispatch(1, 1)
    ag_relay(1, 2, 0)
    turn_weights(2)
    ag_relay(1, 2, 1)
    dispatch(1, 6)
    dispatch(1, 2)
    turn_weights(3)
    ag_relay(1, 3, 0)
    ag_relay(1, 3, 1)
    dispatch(1, 5)
    dispatch(1, 3)
    rs(0, 0)
    rs(0, 1)
    backward(0)
    ag_relay(1, 4, 0)
    dispatch(1, 4)
    give_back(1, 0)
    backward(1)
    give_back(1, 1)
    rs(0, 2)
    await_rows(1, 2)
    await_rows(1, 3)
    wgrad(1, 2)
    wsend(1, 0)
    wgrad(1, 3)
    wsend(1, 4)
    rs(0, 3)
    backward(2)
    give_back(1, 2)
    backward(3)
    give_back(1, 3)
    rs(0, 4)
    wgrad(0, 2)
    wsend(0, 0)
    wgrad(0, 3)
    wsend(0, 4)
    wsend(1, 3)
    wsend(0, 3)
    rs(0, 5)
    wgrad(1, 1)
    wchain(1, 0)
    rs(0, 6)
    wgrad(0, 1)
    rs(1, 0)
    rs(1, 1)
    wgrad(1, 0)
    wchain(0, 0)
    wsend(1, 1)
    wsend(0, 1)
    rs_end(0, mixed_v)
    out_copy("mixed", mixed_v, mixed_o, 0)
    wgrad(0, 0)
    for r in (4, 3):
        gate_grad(r)
    rs(1, 2)
    wchain(1, 1)
    for r in (5, 2):
        gate_grad(r)
    rs(1, 3)
    wfar(1)
    for r in (6, 1):
        gate_grad(r)
    rs(1, 4)
    for r in (7, 0):
        gate_grad(r)
    wchain(0, 1)
    wfar(0)
    rs(1, 5)
    rs(1, 6)
    rcopy(gg_send.at[1:8], gg_recv.at[1:8], gg_s.at[0], gg_r.at[0], along_z(1)).wait_recv()
    gg = gg_recv[0, 0:4, :]
    for r in range(1, 8):
        gg = gg + gg_recv[r, 0:4, :]
    gg_v[...] = gg
    out_copy("gg", gg_v, gg_o, 2)
    wend(1, gout_v)
    out_copy("gout", gout_v, gout_o, 4)
    rs_end(1, tgrad_v)
    out_copy("tgrad", tgrad_v, tgrad_o, 1)
    wend(0, gin_v)
    out_copy("gin", gin_v, gin_o, 3)
    for ref, sem in (
        (rs_send, ag_s), (metall.at[1:8], meta_s), (disp, disp_s), (disp, ret_s), (rs_send, rs_s),
        (gg_send.at[1:8], gg_s), (wx_send, wx_s), (wy_send, wy_s),
    ):
        rcopy(ref, ref, sem.at[0], wy_r.at[0], y_far).wait_send()
    for name in ("mixed", "gg", "gout", "tgrad", "gin"):
        local[name].wait()


def hand_on(*refs):
    ins, outs, vms, sems = refs[:5], refs[5:10], refs[10:15], refs[15]
    loads = [pltpu.make_async_copy(ins[i], vms[i], sems.at[0, i]) for i in range(5)]
    stores = [pltpu.make_async_copy(vms[i], outs[i], sems.at[1, i]) for i in range(5)]
    for load in loads:
        load.start()
    for load, store in zip(loads, stores):
        load.wait()
        store.start()
    for store in stores:
        store.wait()


def body(tokens, expert_ids, gate_probs, out_grad, w_in, w_out):
    anyspec = pl.BlockSpec(memory_space=pl.ANY)
    dma = pltpu.SemaphoreType.DMA
    scratch = [
        pltpu.VMEM((4, T), jnp.int32),
        pltpu.VMEM((4, T), F32),
        pltpu.VMEM((2, 8, T, D), BF),
        pltpu.VMEM((8, 8, T), F32),
        pltpu.VMEM((8, T, T), BF),
        pltpu.VMEM((8, T, T), BF),
        pltpu.VMEM((8, T, T), BF),
        pltpu.VMEM((8, T, T), F32),
        pltpu.VMEM((D, D), BF),
        pltpu.VMEM((D, D), BF),
        pltpu.VMEM((D, D), BF),
        pltpu.VMEM((D, D), BF),
        pltpu.VMEM((2, 8, 3, CAP, D), BF),
        pltpu.VMEM((2, 8, 4, CAP, D), BF),
        pltpu.VMEM((D, 1024), BF),
        pltpu.VMEM((D, 1024), BF),
        pltpu.VMEM((1024, D), F32),
        pltpu.VMEM((1024, D), BF),
        pltpu.VMEM((2, 8, 4, CAP, D), BF),
        pltpu.VMEM((2, 8, 4, CAP, D), BF),
        pltpu.VMEM((T, D), BF),
        pltpu.VMEM((T, D), BF),
        pltpu.VMEM((4, T), F32),
        pltpu.VMEM((128, D), F32),
        pltpu.VMEM((128, D), F32),
        pltpu.VMEM((256, D), BF),
        pltpu.VMEM((2, 2, 7, HALF, D), BF),
        pltpu.VMEM((2, 2, 7, HALF, D), BF),
        pltpu.VMEM((8, 8, T), F32),
        pltpu.VMEM((8, 8, T), F32),
        pltpu.VMEM((2, 6, 128, D), BF),
        pltpu.VMEM((2, 6, 128, D), BF),
        pltpu.VMEM((2, 2, 128, D), F32),
        pltpu.VMEM((2, 2, 128, D), F32),
        pltpu.VMEM((2, 128, D), BF),
        pltpu.VMEM((2, 128, D), BF),
        dma((11,)),
        dma((1,)), dma((2, 4, 2)),
        dma((1,)), dma((2, 4)),
        dma((1,)), dma((2, 4)),
        dma((1,)), dma((2, 8)),
        dma((1,)), dma((2, 7)),
        dma((1,)), dma((1,)),
        dma((1,)), dma((2, 6)),
        dma((1,)), dma((2,)),
    ]
    shapes = (
        jax.ShapeDtypeStruct((T, D), BF),
        jax.ShapeDtypeStruct((T, D), BF),
        jax.ShapeDtypeStruct((4, T), F32),
        jax.ShapeDtypeStruct((128, D), F32),
        jax.ShapeDtypeStruct((128, D), F32),
    )
    results = pl.pallas_call(
        kernel,
        out_shape=shapes,
        in_specs=[anyspec] * 6,
        out_specs=(anyspec,) * 5,
        scratch_shapes=scratch,
        compiler_params=pltpu.CompilerParams(
            collective_id=0, has_side_effects=True, vmem_limit_bytes=63 * 1024 * 1024
        ),
        cost_estimate=pl.CostEstimate(
            flops=14_000_000_000, bytes_accessed=8_000_000, transcendentals=2_000_000
        ),
    )(tokens, out_grad, expert_ids.T, gate_probs.T, w_in, w_out)
    mixed, tgrad, gg, gin, gout = pl.pallas_call(
        hand_on,
        out_shape=shapes,
        in_specs=[anyspec] * 5,
        out_specs=(anyspec,) * 5,
        scratch_shapes=[pltpu.VMEM(shape.shape, shape.dtype) for shape in shapes] + [dma((2, 5))],
    )(*results)
    return mixed, tgrad, gg.T, gin[None], gout[None]


def solution(mesh):
    token = P(("rep", "ep"), None)
    weight = P("ep", None, None)
    return jax.shard_map(
        body,
        mesh=mesh,
        in_specs=(token, token, token, token, weight, weight),
        out_specs=(token, token, token, P("ep", "rep", None), P("ep", "rep", None)),
        check_vma=False,
    )
```

```python
import jax
import jax.numpy as jnp
from jax import lax
from jax.experimental import pallas as pl
from jax.experimental.pallas import tpu as pltpu
from jax.sharding import PartitionSpec as P

MESH = pl.DeviceIdType.MESH
BF = jnp.bfloat16
F32 = jnp.float32
NZ, NX = 8, 4
T = 128
HALF = 64
CAP = 32
D = 1024
LOG2_E = 1.4426950408889634
INV_ROOT_TAU = 0.3989422804014327
ERF_P = 0.3275911
ERF_A = (0.254829592, -0.284496736, 1.421413741, -1.453152027, 1.061405429)
ROOT_HALF = 0.7071067811865476

ORDER = (0, 7, 1, 6, 2, 5, 3, 4)
POS = {r: p for p, r in enumerate(ORDER)}
RS_UNITS = (
    ((0, 4), (1, 3), (0, 3), (1, 2), (0, 2), (1, 1), (0, 1)),
    ((1, 4), (0, 5), (1, 5), (0, 6), (1, 6), (0, 7), (1, 7)),
)


def dot(a, b, dims=((1,), (0,))):
    return lax.dot_general(a, b, (dims, ((), ())), preferred_element_type=F32)


def gelu_parts(v):
    bell = jnp.exp2(v * v * (-0.5 * LOG2_E))
    base = 1.0 + jnp.abs(v) * (ERF_P * ROOT_HALF)
    t = pl.reciprocal(base, approx=True)
    t = t * (2.0 - base * t)
    poly = 0.5 * ERF_A[4]
    for a in ERF_A[3::-1]:
        poly = poly * t + 0.5 * a
    tail = poly * t * bell
    return jnp.where(v < 0.0, tail, 1.0 - tail), v * bell * INV_ROOT_TAU


def kernel(
    tok, grd, ids_o, gates_o, win, wout,
    mixed_o, tgrad_o, gg_o, gin_o, gout_o,
    ids, gates, ball, metall, sel, selt, gatet, gslot, wi, wo, wit, wot,
    disp, arr, arrt, actt, slope, pre, res, ret,
    mixed_v, tgrad_v, gg_v, gin_v, gout_v, hid,
    rs_send, rs_recv, gg_send, gg_recv,
    wx_send, wx_recv, wx_own, wx_chain, wy_send, wy_recv,
    loc_sem, ag_s, ag_r, meta_s, meta_r, disp_s, disp_r, ret_s, ret_r,
    rs_s, rs_r, gg_s, gg_r, wx_s, wx_r, wy_s, wy_r,
):
    rep = lax.axis_index("rep")
    ep = lax.axis_index("ep")
    x, y_hi = lax.rem(rep, 4), lax.div(rep, 4)
    c, y_lo, z = lax.rem(ep, 2), lax.rem(lax.div(ep, 2), 2), lax.div(ep, 4)
    y = y_hi * 2 + y_lo

    def dev(x_, y_, z_, c_):
        return (lax.div(y_, 2) * 4 + x_, (z_ * 2 + lax.rem(y_, 2)) * 2 + c_)

    def along_z(r):
        return dev(x, y, lax.rem(z + r, 8), c)

    y_up, y_dn = lax.rem(y + 1, 4), lax.rem(y + 3, 4)
    y_to = lax.rem(y + 1 + 2 * c, 4)
    y_from_other = lax.rem(y + 1 + 2 * c, 4)
    y_from_same = lax.rem(y + 3 - 2 * c, 4)
    other = 1 - c
    to_plane = (None, dev(x, y, z, other), dev(x, y_to, z, c), dev(x, y_to, z, other))
    from_plane = (
        None, dev(x, y, z, other), dev(x, y_from_same, z, c), dev(x, y_from_other, z, other),
    )
    x_right, x_left = dev(lax.rem(x + 1, 4), y, z, c), dev(lax.rem(x + 3, 4), y, z, c)
    y_far = dev(x, lax.rem(y + 2, 4), z, c)
    partners = [along_z(1), along_z(7)]
    partners += [to_plane[1], to_plane[2], to_plane[3], from_plane[2]]
    partners += [x_right, x_left]

    def rcopy(src, dst, ss, rs, device):
        return pltpu.make_async_remote_copy(
            src_ref=src, dst_ref=dst, send_sem=ss, recv_sem=rs, device_id=device, device_id_type=MESH
        )

    def go(copy):
        copy.start()

    local = {}

    def lcopy(name, src, dst, i):
        local[name] = pltpu.make_async_copy(src, dst, loc_sem.at[i])
        local[name].start()


    def out_copy(name, src, dst, i):
        lcopy(name, src, dst, 5 + i)

    barrier = pltpu.get_barrier_semaphore()
    for p in partners:
        pl.semaphore_signal(barrier, inc=1, device_id=p, device_id_type=MESH)
    lcopy("ids", ids_o, ids, 2)
    lcopy("gates", gates_o, gates, 10)
    lcopy("x", tok, ball.at[0, 0], 0)
    lcopy("wi", win.at[0], wi, 3)
    lcopy("wo", wout.at[0], wo, 4)
    lcopy("g", grd, ball.at[1, 0], 1)
    pl.semaphore_wait(barrier, len(partners))

    own = (tok, grd)

    def ag(a, d, h, half):
        rows = pl.ds(half * HALF, HALF)
        if h == 1:
            src = own[a].at[rows]
        else:
            src = ball.at[a, 8 - (h - 1) if d == 0 else h - 1, rows]
        dst = ball.at[a, 8 - h if d == 0 else h, rows]
        return rcopy(src, dst, ag_s.at[0], ag_r.at[a, h - 1, 0 if half == d else 1],
                     along_z(1 if d == 0 else 7))

    def ag_own(a):
        for i in range(2):
            go(ag(a, 0, 1, i))
            go(ag(a, 1, 1, 1 - i))

    def ag_relay(a, h, i):
        rcopy(ball.at[a, 0], ball.at[a, 0], ag_s.at[0], ag_r.at[a, h - 1, i], along_z(1)).wait_recv()
        for d in range(2):
            if h < (4 if i == 0 else 3):
                go(ag(a, d, h + 1, d if i == 0 else 1 - d))

    def meta_copy(d, h):
        src, dst = (8 - (h - 1), 8 - h) if d == 0 else (h - 1, h)
        return rcopy(metall.at[src % 8], metall.at[dst], meta_s.at[0], meta_r.at[d, h - 1],
                     along_z(1 if d == 0 else 7))

    def meta_relay(h):
        for d in range(2 if h < 4 else 1):
            meta_copy(d, h).wait_recv()
            if h < (4 if d == 0 else 3):
                go(meta_copy(d, h + 1))

    ag_own(0)

    local["ids"].wait()
    local["gates"].wait()
    expert = lax.broadcasted_iota(jnp.int32, (32, T), 0)
    named = [jnp.where(ids[k:k + 1, :] == expert, 1.0, 0.0) for k in range(4)]
    earlier = jnp.where(
        lax.broadcasted_iota(jnp.int32, (T, T), 0) < lax.broadcasted_iota(jnp.int32, (T, T), 1), 1.0, 0.0
    ).astype(BF)
    before = dot((named[0] + named[1] + named[2] + named[3]).astype(BF), earlier)
    for k in range(4):
        metall[0, k:k + 1, :] = (
            ids[k:k + 1, :].astype(F32) * CAP + jnp.sum(named[k] * before, axis=0, keepdims=True)
        )
    metall[0, 4:8, :] = gates[...]
    for d in range(2):
        go(meta_copy(d, 1))

    row = lax.broadcasted_iota(jnp.int32, (T, T), 0)
    q = lax.div(row, CAP)
    q_c = lax.rem(c + lax.rem(q, 2), 2)
    q_y = lax.rem(y_lo + lax.div(q, 2), 2)
    row_place = (((z * 2 + q_y) * 2 + q_c) * CAP + lax.rem(row, CAP)).astype(F32)

    def onehots(r):
        m = metall[r]
        return [jnp.where(m[k:k + 1, :] == row_place, 1.0, 0.0) for k in range(4)], m

    def build(r):
        hots, m = onehots(r)
        total = hots[0] + hots[1] + hots[2] + hots[3]
        gated = sum(hots[k] * m[4 + k:5 + k, :] for k in range(4))
        sel[r] = total.astype(BF)
        selt[r] = total.T.astype(BF)
        gatet[r] = gated.T.astype(BF)
        gslot[r] = jnp.broadcast_to(jnp.sum(gated, axis=1, keepdims=True), (T, T))

    def disp_copy(a, r, k):
        p = POS[r]
        return rcopy(disp.at[a, p, k - 1], arr.at[a, p, k], disp_s.at[0], disp_r.at[a, p // 2],
                     to_plane[k])

    def dispatch(a, r):
        if r == 0:
            local["x" if a == 0 else "g"].wait()
        rows = dot(sel[r], ball[a, r])
        if a == 1:
            rows = rows * gslot[r][:, 0:1]
        rows = rows.astype(BF)
        p = POS[r]
        for k in (2, 3, 1):
            disp[a, p, k - 1] = rows[k * CAP:(k + 1) * CAP]
            go(disp_copy(a, r, k))
        arr[a, p, 0] = rows[:CAP]

    def ret_copy(a, p, k):
        return rcopy(res.at[a, p, k], ret.at[a, p, k], ret_s.at[0], ret_r.at[a, p],
                     from_plane[k])

    def give_back(a, j):
        for p in (2 * j, 2 * j + 1):
            for k in (2, 3, 1):
                go(ret_copy(a, p, k))
            ret[a, p, 0] = res[a, p, 0]

    awaited = set()

    def await_rows(a, j):
        if (a, j) in awaited:
            return
        awaited.add((a, j))
        two = disp.at[a, 2 * j:2 * j + 2]
        rcopy(two, two, disp_s.at[0], disp_r.at[a, j], to_plane[1]).wait_recv()

    def turn_weights(n):
        rows = pl.ds(n * 256, 256)
        wit[:, rows] = wi[rows, :].T
        wot[:, rows] = wo[rows, :].T

    def forward_a(j):
        await_rows(0, j)
        rows = arr[0, 2 * j:2 * j + 2].reshape(256, D)
        span = pl.ds(256 * j, 256)
        acts = []
        for n in range(4):
            cols = pl.ds(n * 256, 256)
            v = dot(rows, wi[:, cols])
            below, dense = gelu_parts(v)
            slope[span, cols] = below + dense
            acts.append((v * below).astype(BF))
            actt[cols, span] = acts[-1].T
        hid[...] = jnp.concatenate(acts, axis=1)

    def forward_b(j):
        span = pl.ds(256 * j, 256)
        hidden = hid[...]
        for n in range(4):
            cols = pl.ds(n * 256, 256)
            res[0, 2 * j:2 * j + 2, :, :, cols] = (
                dot(hidden, wo[:, cols]).astype(BF).reshape(2, 4, CAP, 256)
            )
        arrt[:, span] = arr[0, 2 * j:2 * j + 2].reshape(256, D).T

    def backward_a(j):
        await_rows(1, j)
        rows = arr[1, 2 * j:2 * j + 2].reshape(256, D)
        span = pl.ds(256 * j, 256)
        for n in range(4):
            cols = pl.ds(n * 256, 256)
            pre[span, cols] = (dot(rows, wot[:, cols]) * slope[span, cols]).astype(BF)

    def backward_b(j):
        hidden = pre[pl.ds(256 * j, 256), :]
        for n in range(4):
            cols = pl.ds(n * 256, 256)
            res[1, 2 * j:2 * j + 2, :, :, cols] = (
                dot(hidden, wit[:, cols]).astype(BF).reshape(2, 4, CAP, 256)
            )

    returned = set()

    def combine(a, r, half):
        p = POS[r]
        if (a, p) not in returned:
            returned.add((a, p))
            rcopy(disp.at[a, p], disp.at[a, p], ret_s.at[0], ret_r.at[a, p], to_plane[1]).wait_recv()
        weights = (gatet if a == 0 else selt)[r, half * HALF:(half + 1) * HALF]
        return dot(weights, ret[a, p].reshape(T, D))

    def rs_copy(a, d, i):
        return rcopy(rs_send.at[a, d, i], rs_recv.at[a, d, i], rs_s.at[0], rs_r.at[a, i],
                     along_z(1 if d == 0 else 7))

    def rs_await(a, n):
        rcopy(ball.at[a, 0], ball.at[a, 0], rs_s.at[0], rs_r.at[a, n], along_z(1)).wait_recv()

    def rs(a, i):
        totals = [combine(a, r, half) for half, r in (RS_UNITS[0][i], RS_UNITS[1][i])]
        if i >= 2:
            rs_await(a, i - 2)
        for d in range(2):
            total = totals[d]
            if i >= 2:
                total = total + rs_recv[a, d, i - 2].astype(F32)
            rs_send[a, d, i] = total.astype(BF)
            go(rs_copy(a, d, i))

    def rs_end(a, out):
        totals = [combine(a, 0, half) for half in range(2)]
        rs_await(a, 5)
        rs_await(a, 6)
        for half in range(2):
            total = totals[half]
            for d in range(2):
                n = RS_UNITS[d].index((half, 1 if d == 0 else 7))
                total = total + rs_recv[a, d, n].astype(F32)
            out[half * HALF:(half + 1) * HALF, :] = total.astype(BF)

    def gg_copy(r):
        return rcopy(gg_send.at[r], gg_recv.at[r], gg_s.at[0], gg_r.at[0], along_z(r))

    def gate_grad(r):
        m = dot(ret[0, POS[r]].reshape(T, D), ball[1, r], ((1,), (1,)))
        hots, _ = onehots(r)
        out = gg_send if r else gg_recv
        for k in range(4):
            out[r, k:k + 1, :] = jnp.sum(m * hots[k], axis=0, keepdims=True)
        if r:
            out[r, 4:8, :] = jnp.zeros((4, T), F32)
            go(gg_copy(r))

    def wx_copy(w, i):
        return rcopy(wx_send.at[w, i], wx_recv.at[w, i], wx_s.at[0], wx_r.at[w, i],
                     x_right if i < 3 else x_left)

    def wgrad(w, dx):
        left = actt if w == 1 else arrt
        dest = lax.rem(x + dx, 4)
        lhs = jnp.concatenate(
            [left[pl.ds(pl.multiple_of((yh * 4 + dest) * 128, 128), 128), :] for yh in (1 - y_hi, y_hi)],
            axis=0,
        )
        for n in range(4):
            cols = pl.ds(n * 256, 256)
            right = arr[1, :, :, :, cols].reshape(1024, 256) if w == 1 else pre[:, cols]
            v = dot(lhs, right)
            far, near = v[:128], v[128:]
            if dx == 2:
                wx_send[w, 0, :, cols] = far.astype(BF)
                wx_send[w, 3, :, cols] = near.astype(BF)
            elif dx == 1:
                wx_send[w, 1, :, cols] = near.astype(BF)
                wx_chain[w, 0, :, cols] = far
            elif dx == 3:
                wx_send[w, 4, :, cols] = far.astype(BF)
                wx_chain[w, 1, :, cols] = near
            else:
                wx_own[w, 0, :, cols] = far
                wx_own[w, 1, :, cols] = near

    def wsend(w, i):
        go(wx_copy(w, i))

    def wchain(w, n):
        i, first = (2, 0) if n == 0 else (5, 3)
        wx_copy(w, first).wait_recv()
        wx_send[w, i] = (wx_chain[w, n] + wx_recv[w, first].astype(F32)).astype(BF)
        go(wx_copy(w, i))

    def wy_copy(w):
        return rcopy(wy_send.at[w], wy_recv.at[w], wy_s.at[0], wy_r.at[w], y_far)

    def wfar(w):
        for i in (2, 4):
            wx_copy(w, i).wait_recv()
        total = wx_own[w, 0] + wx_recv[w, 2].astype(F32) + wx_recv[w, 4].astype(F32)
        wy_send[w] = total.astype(BF)
        go(wy_copy(w))

    def wend(w, out):
        wy_copy(w).wait_recv()
        wx_copy(w, 1).wait_recv()
        total = wx_own[w, 1] + wx_recv[w, 1].astype(F32) + wy_recv[w].astype(F32)
        wx_copy(w, 5).wait_recv()
        out[...] = total + wx_recv[w, 5].astype(F32)

    def backward(j):
        backward_a(j)
        backward_b(j)

    build(0)
    dispatch(0, 0)
    local["wi"].wait()
    local["wo"].wait()
    turn_weights(0)
    ag_relay(0, 1, 0)
    meta_relay(1)
    build(7)
    build(1)
    turn_weights(1)
    ag_relay(0, 1, 1)
    dispatch(0, 7)
    dispatch(0, 1)
    ag_relay(0, 2, 0)
    meta_relay(2)
    build(6)
    build(2)
    ag_relay(0, 2, 1)
    dispatch(0, 6)
    dispatch(0, 2)
    forward_a(0)
    ag_relay(0, 3, 0)
    ag_own(1)
    meta_relay(3)
    build(5)
    build(3)
    forward_b(0)
    give_back(0, 0)
    ag_relay(0, 3, 1)
    dispatch(0, 5)
    dispatch(0, 3)
    forward_a(1)
    meta_relay(4)
    build(4)
    ag_relay(0, 4, 0)
    dispatch(0, 4)
    forward_b(1)
    give_back(0, 1)
    ag_relay(1, 1, 0)
    forward_a(2)
    forward_b(2)
    give_back(0, 2)
    ag_relay(1, 1, 1)
    forward_a(3)
    forward_b(3)
    give_back(0, 3)
    dispatch(1, 0)
    dispatch(1, 7)
    dispatch(1, 1)
    ag_relay(1, 2, 0)
    turn_weights(2)
    ag_relay(1, 2, 1)
    dispatch(1, 6)
    dispatch(1, 2)
    turn_weights(3)
    ag_relay(1, 3, 0)
    ag_relay(1, 3, 1)
    dispatch(1, 5)
    dispatch(1, 3)
    rs(0, 0)
    rs(0, 1)
    backward(0)
    ag_relay(1, 4, 0)
    dispatch(1, 4)
    backward(1)
    rs(0, 2)
    await_rows(1, 2)
    await_rows(1, 3)
    wgrad(1, 2)
    wsend(1, 0)
    wgrad(1, 3)
    wsend(1, 4)
    give_back(1, 0)
    give_back(1, 1)
    rs(0, 3)
    backward(2)
    give_back(1, 2)
    backward(3)
    give_back(1, 3)
    rs(0, 4)
    wgrad(0, 2)
    wsend(0, 0)
    wgrad(0, 3)
    wsend(0, 4)
    wsend(1, 3)
    wsend(0, 3)
    rs(0, 5)
    wgrad(1, 1)
    wchain(1, 0)
    rs(0, 6)
    wgrad(0, 1)
    rs(1, 0)
    rs(1, 1)
    wgrad(1, 0)
    wchain(0, 0)
    wsend(1, 1)
    wsend(0, 1)
    rs_end(0, mixed_v)
    out_copy("mixed", mixed_v, mixed_o, 0)
    wgrad(0, 0)
    for r in (4, 3):
        gate_grad(r)
    rs(1, 2)
    wchain(1, 1)
    for r in (5, 2):
        gate_grad(r)
    rs(1, 3)
    wfar(1)
    for r in (6, 1):
        gate_grad(r)
    rs(1, 4)
    for r in (7, 0):
        gate_grad(r)
    wchain(0, 1)
    wfar(0)
    rs(1, 5)
    rs(1, 6)
    rcopy(gg_send.at[1:8], gg_recv.at[1:8], gg_s.at[0], gg_r.at[0], along_z(1)).wait_recv()
    gg = gg_recv[0, 0:4, :]
    for r in range(1, 8):
        gg = gg + gg_recv[r, 0:4, :]
    gg_v[...] = gg
    out_copy("gg", gg_v, gg_o, 2)
    wend(1, gout_v)
    out_copy("gout", gout_v, gout_o, 4)
    rs_end(1, tgrad_v)
    out_copy("tgrad", tgrad_v, tgrad_o, 1)
    wend(0, gin_v)
    out_copy("gin", gin_v, gin_o, 3)
    for ref, sem in (
        (rs_send, ag_s), (metall.at[1:8], meta_s), (disp, disp_s), (disp, ret_s), (rs_send, rs_s),
        (gg_send.at[1:8], gg_s), (wx_send, wx_s), (wy_send, wy_s),
    ):
        rcopy(ref, ref, sem.at[0], wy_r.at[0], y_far).wait_send()
    for name in ("mixed", "gg", "gout", "tgrad", "gin"):
        local[name].wait()


def hand_on(*refs):
    ins, outs, vms, sems = refs[:5], refs[5:10], refs[10:15], refs[15]
    loads = [pltpu.make_async_copy(ins[i], vms[i], sems.at[0, i]) for i in range(5)]
    stores = [pltpu.make_async_copy(vms[i], outs[i], sems.at[1, i]) for i in range(5)]
    for load in loads:
        load.start()
    for load, store in zip(loads, stores):
        load.wait()
        store.start()
    for store in stores:
        store.wait()


def body(tokens, expert_ids, gate_probs, out_grad, w_in, w_out):
    anyspec = pl.BlockSpec(memory_space=pl.ANY)
    dma = pltpu.SemaphoreType.DMA
    scratch = [
        pltpu.VMEM((4, T), jnp.int32),
        pltpu.VMEM((4, T), F32),
        pltpu.VMEM((2, 8, T, D), BF),
        pltpu.VMEM((8, 8, T), F32),
        pltpu.VMEM((8, T, T), BF),
        pltpu.VMEM((8, T, T), BF),
        pltpu.VMEM((8, T, T), BF),
        pltpu.VMEM((8, T, T), F32),
        pltpu.VMEM((D, D), BF),
        pltpu.VMEM((D, D), BF),
        pltpu.VMEM((D, D), BF),
        pltpu.VMEM((D, D), BF),
        pltpu.VMEM((2, 8, 3, CAP, D), BF),
        pltpu.VMEM((2, 8, 4, CAP, D), BF),
        pltpu.VMEM((D, 1024), BF),
        pltpu.VMEM((D, 1024), BF),
        pltpu.VMEM((1024, D), F32),
        pltpu.VMEM((1024, D), BF),
        pltpu.VMEM((2, 8, 4, CAP, D), BF),
        pltpu.VMEM((2, 8, 4, CAP, D), BF),
        pltpu.VMEM((T, D), BF),
        pltpu.VMEM((T, D), BF),
        pltpu.VMEM((4, T), F32),
        pltpu.VMEM((128, D), F32),
        pltpu.VMEM((128, D), F32),
        pltpu.VMEM((256, D), BF),
        pltpu.VMEM((2, 2, 7, HALF, D), BF),
        pltpu.VMEM((2, 2, 7, HALF, D), BF),
        pltpu.VMEM((8, 8, T), F32),
        pltpu.VMEM((8, 8, T), F32),
        pltpu.VMEM((2, 6, 128, D), BF),
        pltpu.VMEM((2, 6, 128, D), BF),
        pltpu.VMEM((2, 2, 128, D), F32),
        pltpu.VMEM((2, 2, 128, D), F32),
        pltpu.VMEM((2, 128, D), BF),
        pltpu.VMEM((2, 128, D), BF),
        dma((11,)),
        dma((1,)), dma((2, 4, 2)),
        dma((1,)), dma((2, 4)),
        dma((1,)), dma((2, 4)),
        dma((1,)), dma((2, 8)),
        dma((1,)), dma((2, 7)),
        dma((1,)), dma((1,)),
        dma((1,)), dma((2, 6)),
        dma((1,)), dma((2,)),
    ]
    shapes = (
        jax.ShapeDtypeStruct((T, D), BF),
        jax.ShapeDtypeStruct((T, D), BF),
        jax.ShapeDtypeStruct((4, T), F32),
        jax.ShapeDtypeStruct((128, D), F32),
        jax.ShapeDtypeStruct((128, D), F32),
    )
    results = pl.pallas_call(
        kernel,
        out_shape=shapes,
        in_specs=[anyspec] * 6,
        out_specs=(anyspec,) * 5,
        scratch_shapes=scratch,
        compiler_params=pltpu.CompilerParams(
            collective_id=0, has_side_effects=True, vmem_limit_bytes=63 * 1024 * 1024
        ),
        cost_estimate=pl.CostEstimate(
            flops=14_000_000_000, bytes_accessed=8_000_000, transcendentals=2_000_000
        ),
    )(tokens, out_grad, expert_ids.T, gate_probs.T, w_in, w_out)
    mixed, tgrad, gg, gin, gout = pl.pallas_call(
        hand_on,
        out_shape=shapes,
        in_specs=[anyspec] * 5,
        out_specs=(anyspec,) * 5,
        scratch_shapes=[pltpu.VMEM(shape.shape, shape.dtype) for shape in shapes] + [dma((2, 5))],
    )(*results)
    return mixed, tgrad, gg.T, gin[None], gout[None]


def solution(mesh):
    token = P(("rep", "ep"), None)
    weight = P("ep", None, None)
    return jax.shard_map(
        body,
        mesh=mesh,
        in_specs=(token, token, token, token, weight, weight),
        out_specs=(token, token, token, P("ep", "rep", None), P("ep", "rep", None)),
        check_vma=False,
    )
```
